256 devices in a mesh: dp: 32 (over z_lo, y, core), section: 8 (over z_hi, x).
Axes of the slice: x: 4, y: 4, z: 8 (z_hi: 2, z_lo: 4; z = z_hi * 4 + z_lo), core: 2. Of those that a mesh axis runs over, the one named last changes fastest.
Arguments:
- first_input: bfloat16 [8192, 2048], P('dp'), may hold values from -6 to 6
- upstream: bfloat16 [8192, 2048], P('dp'), may hold values from -6 to 6
- history: bfloat16 [8, 2, 128, 64, 2048], P('section', None, 'dp'), as said below
- example_ids: int32 [32, 4], P('dp'), may hold values from 0 to 3, each once within a row
- norm_gain: float32 [8, 2048], P('section'), may hold values from 0.1 to 1.9
- weight: bfloat16 [8, 2048, 2048], P('section', 'dp'), may hold values from -0.125 to 0.125
Outputs:
- section_outputs: bfloat16 [8, 8192, 2048], P('section', 'dp')
- block_scales: bfloat16 [8, 8192, 16], P('section', 'dp')
- weight_grad: float32 [8, 2048, 2048], P('section', 'dp')
- gain_grad: float32 [8, 2048], P('section')
The draws below stay inside these ranges and needn't reach their ends.
Inputs may be any that keep to these rules, and one draw needn't show every extreme that they name: `example_ids`: each row names each stored example of its replica once. history[s, 1] equals history[s - 1, 0], indices of the first dimension taken modulo 8.
All inputs are finite; a program needn't handle non-finite values. Where the reference program divides by a largest or mean magnitude, that divisor is 1e-20 or more.
Results may differ from the reference program's by a relative error of at most 0.038.
Values may be sent and summed in bfloat16 or wider, within the bound.
A program may use at most 64 MiB of HBM per device.

```python
import jax
import jax.numpy as jnp
from jax import lax

D = 2048
SEQ = 64
BLOCK = 128
POOL = 4
TOK_DEV = 256
TOKENS = 8192
POOL_ALL = 128
N_DP = 32
N_SECTION = 8


def draw_history(key, part):
    key = jax.random.fold_in(key, 11)
    shape = (N_SECTION, POOL_ALL, SEQ, D)
    base = jax.random.normal(key, shape, jnp.float32)
    paired = jnp.stack([base, jnp.roll(base, 1, axis=0)], axis=1)
    return paired.astype(jnp.bfloat16)


def raised(values, stream_key, source, target, shards_of, factor):
    owner, partner = [(jnp.arange(values.shape[position]) // (values.shape[position] // shards_of)).reshape([-1 if axis == position else 1 for axis in range(values.ndim)]) for position in (source, target)]
    chosen = jax.random.permutation(stream_key, shards_of)[partner]
    strong = (owner == chosen) | (owner == (partner + shards_of // 2) % shards_of)
    return jnp.where(strong, factor * values, values)


def level_of(stream_key, dims, split, low, high):
    def one(position, blocks):
        draws = jax.random.uniform(jax.random.fold_in(jax.random.fold_in(stream_key, 6), position), (blocks,), jnp.float32, low / len(split), high / len(split))
        return jnp.repeat(jnp.exp(draws), dims[position] // blocks).reshape((-1,) + (1,) * (len(dims) - position - 1))

    loudness = one(*split[0])
    for cut in split[1:]:
        loudness = loudness * one(*cut)
    return loudness


def gaussian(own_key, extent, scale, most, shards=(), kind=jnp.bfloat16):
    values = jax.random.normal(own_key, extent, jnp.float32) * scale
    if len(shards) > 0:
        values = level_of(own_key, extent, shards, -0.22, 0.18) * values
    return jnp.clip(values, min=-most, max=most).astype(kind)


def heavy_noise(key, dims, scale, limit, cuts, heavy, held_as=jnp.bfloat16):
    values = scale * jax.random.normal(key, dims, jnp.float32)
    if cuts:
        values = values * level_of(key, dims, cuts, -0.22, 0.18)
    return jnp.clip(raised(values, jax.random.fold_in(key, 3), *heavy), -limit, limit).astype(held_as)


def setup_inputs(seed: int = 0) -> dict:
    streams_of = jax.random.split(jax.random.key(seed), 7)
    return {
        "first_input": heavy_noise(streams_of[0], (TOKENS, D), 1.0, 6.0, ((0, 32),), (0, 1, 32, 2.75)),
        "upstream": gaussian(streams_of[1], (TOKENS, D), 1.0, 6.0, ((0, 32),)),
        "history": draw_history(jax.random.fold_in(streams_of[6], 71), 0),
        "example_ids": jax.vmap(lambda own: jax.random.permutation(own, POOL))(jax.random.split(streams_of[3], N_DP)).reshape((N_DP, POOL)).astype(jnp.int32),
        "norm_gain": jnp.clip(1.0 + 0.18 * jax.random.normal(streams_of[4], (N_SECTION, D), jnp.float32), 0.1, 1.9),
        "weight": gaussian(streams_of[5], (N_SECTION, D, D), D ** -0.5, 0.125, ((0, 8), (1, 32))),
    }


def encode_blocks(values):
    rows, width = values.shape
    blocks = values.reshape(rows, width // BLOCK, BLOCK)
    scale = (lax.optimization_barrier(jnp.max(jnp.abs(blocks), axis=-1)) + 1e-06).astype(jnp.bfloat16)
    coded = (blocks / scale.astype(jnp.float32)[..., None]).astype(jnp.bfloat16)
    return (coded.reshape(rows, width), scale)

def decode_blocks(coded, scale):
    rows, width = coded.shape
    blocks = coded.astype(jnp.float32).reshape(rows, width // BLOCK, BLOCK)
    return (blocks * scale.astype(jnp.float32)[..., None]).reshape(rows, width)

def layer_forward(inputs, gain_row, weight_full):
    values = inputs.astype(jnp.float32)
    inverse = lax.rsqrt(lax.optimization_barrier(jnp.mean(values * values, axis=-1, keepdims=True)) + 1e-05)
    normed = (values * inverse * gain_row).astype(jnp.bfloat16)
    mixed = jnp.dot(normed, weight_full, preferred_element_type=jnp.float32)
    return (values + mixed * jax.nn.sigmoid(mixed)).astype(jnp.bfloat16)

def layer_backward(inputs, gain_row, weight_full, grad_out):
    values = inputs.astype(jnp.float32)
    inverse = lax.rsqrt(lax.optimization_barrier(jnp.mean(values * values, axis=-1, keepdims=True)) + 1e-05)
    unit = values * inverse
    normed = (unit * gain_row).astype(jnp.bfloat16)
    mixed = jnp.dot(normed, weight_full, preferred_element_type=jnp.float32)
    sigma = jax.nn.sigmoid(mixed)
    dmixed = (grad_out * sigma * (1.0 + mixed * (1.0 - sigma))).astype(jnp.bfloat16)
    dnormed = jnp.dot(dmixed, weight_full.T, preferred_element_type=jnp.float32)
    dgain = lax.optimization_barrier(jnp.sum(dnormed * unit, axis=0))
    dunit = dnormed * gain_row
    dinput = grad_out + inverse * (dunit - unit * lax.optimization_barrier(jnp.mean(dunit * unit, axis=-1, keepdims=True)))
    return (dinput, normed, dmixed, dgain)

def reference(first_input, upstream, history, example_ids, norm_gain, weight):
    replicas = example_ids.shape[0]
    rows_index = (jnp.arange(replicas, dtype=jnp.int32)[:, None] * POOL + example_ids).reshape(-1).astype(jnp.int32)

    def stored(section_index, slot):
        return jnp.take(history[section_index, slot], rows_index, axis=0).reshape(TOKENS, D)
    inputs_list = []
    outputs_list = []
    scales_list = []
    current = first_input
    for section_index in range(N_SECTION):
        inputs_list.append(current)
        result = layer_forward(current, norm_gain[section_index], weight[section_index])
        outputs_list.append(result)
        coded, scale = encode_blocks(result.astype(jnp.float32) - stored(section_index, 0).astype(jnp.float32))
        scales_list.append(scale)
        if section_index + 1 < N_SECTION:
            current = (stored(section_index + 1, 1).astype(jnp.float32) + decode_blocks(coded, scale)).astype(jnp.bfloat16)
    weight_grads = [None] * N_SECTION
    gain_grads = [None] * N_SECTION
    grad_now = upstream.astype(jnp.float32)
    for section_index in reversed(range(N_SECTION)):
        dinput, normed, dmixed, dgain = layer_backward(inputs_list[section_index], norm_gain[section_index], weight[section_index], grad_now)
        gain_grads[section_index] = dgain
        normed_parts = normed.reshape(replicas, TOK_DEV, D)
        dmixed_parts = dmixed.reshape(replicas, TOK_DEV, D)

        def add_replica(total, pair):
            partial_value = jnp.dot(pair[0].T, pair[1], preferred_element_type=jnp.float32).astype(jnp.bfloat16)
            partial_value = lax.optimization_barrier(partial_value)
            return (total + partial_value.astype(jnp.float32), None)
        total, _ = lax.scan(add_replica, jnp.zeros((D, D), jnp.float32), (normed_parts, dmixed_parts))
        weight_grads[section_index] = total
        coded, scale = encode_blocks(dinput)
        grad_now = decode_blocks(coded, scale)
    return (jnp.stack(outputs_list), jnp.stack(scales_list), jnp.stack(weight_grads), jnp.stack(gain_grads))
```

```python
import functools

import jax
import jax.numpy as jnp
from jax import lax
from jax.experimental import pallas as pl
from jax.experimental.pallas import tpu as pltpu
from jax.sharding import PartitionSpec as P

MESH = pl.DeviceIdType.MESH
D = 2048
TOK = 256
SEQ = 64
BLOCK = 128
N_SECTION = 8
NZ = 4
NY = 4
SHARD = 64
ROWS_A = 48
MICRO = 8
MR = TOK // MICRO
COLS = 512
bf16 = jnp.bfloat16
f32 = jnp.float32


def relay_kernel(
    first_hbm, up_hbm, hist_hbm, ids, gain, w_hbm,
    out, scales, normed, dmixed, gain_out,
    weight, hist, x_in, g_in, x_out, g_out, factor, scale_buf, gain_acc,
    local_sem, f_send, f_recv, b_send, b_recv,
    za_recv, ya_recv, yb_recv, zb_recv, pair_recv, ag_send,
):
    dp = lax.axis_index("dp")
    s = lax.axis_index("section")
    zl = dp // 8
    y = lax.rem(dp // 2, NY)
    c = lax.rem(dp, 2)

    def device(zl_, y_, c_):
        return (zl_ * 8 + y_ * 2 + c_, s)

    y_up, y_dn, y_far = lax.rem(y + 1, NY), lax.rem(y + 3, NY), lax.rem(y + 2, NY)
    partner = device(zl, y, 1 - c)
    prev_dev, next_dev = (dp, lax.rem(s + 7, 8)), (dp, lax.rem(s + 1, 8))
    has_prev, has_next = s > 0, s < N_SECTION - 1

    def z_dev(step):
        return device(lax.rem(zl + step + NZ, NZ), y, c)

    def row_of(zl_, y_, c_):
        return pl.multiple_of(((zl_ * NY + y_) * 2 + c_) * SHARD, SHARD)

    own_rows = weight.at[pl.ds(row_of(zl, y, c), SHARD)]
    load_w = pltpu.make_async_copy(w_hbm.at[0], own_rows, local_sem.at[0])
    load_w.start()
    load_hist = pltpu.make_async_copy(hist_hbm.at[0, 0], hist, local_sem.at[1])
    load_hist.start()
    load_first = pltpu.make_async_copy(first_hbm, x_in, local_sem.at[2])
    load_up = pltpu.make_async_copy(up_hbm, g_in, local_sem.at[3])

    @pl.when(jnp.logical_not(has_prev))
    def _():
        load_first.start()

    @pl.when(jnp.logical_not(has_next))
    def _():
        load_up.start()

    barrier = pltpu.get_barrier_semaphore()
    for dev in (partner, device(zl, y_up, c), device(zl, y_dn, c)):
        pl.semaphore_signal(barrier, inc=1, device_id=dev, device_id_type=MESH)
    for dev, there in ((z_dev(-1), zl > 0), (z_dev(1), zl < NZ - 1), (prev_dev, has_prev), (next_dev, has_next)):
        @pl.when(there)
        def _():
            pl.semaphore_signal(barrier, inc=1, device_id=dev, device_id_type=MESH)
    greeted = (
        3 + (zl > 0).astype(jnp.int32) + (zl < NZ - 1).astype(jnp.int32)
        + has_prev.astype(jnp.int32) + has_next.astype(jnp.int32)
    )
    pl.semaphore_wait(barrier, greeted)
    load_w.wait()

    sends = []

    def piece_a(zl_, y_):
        return weight.at[pl.ds(row_of(zl_, y_, c), ROWS_A)]

    def piece_b(zl_, y_):
        return weight.at[pl.ds(pl.multiple_of(row_of(zl_, y_, c) + ROWS_A, 16), SHARD - ROWS_A)]

    def send(ref, recv_sem, dev, cond):
        copy = pltpu.make_async_remote_copy(
            src_ref=ref, dst_ref=ref, send_sem=ag_send.at[len(sends)], recv_sem=recv_sem,
            device_id=dev, device_id_type=MESH,
        )
        sends.append((copy, cond))
        if cond is None:
            copy.start()
        else:
            pl.when(cond)(copy.start)

    def arrived(ref, recv_sem, cond):
        copy = pltpu.make_async_remote_copy(
            src_ref=ref, dst_ref=ref, send_sem=ag_send.at[0], recv_sem=recv_sem,
            device_id=partner, device_id_type=MESH,
        )
        if cond is None:
            copy.wait_recv()
        else:
            pl.when(cond)(copy.wait_recv)

    def both(a, b):
        return b if a is None else jnp.logical_and(a, b)

    def in_line(z_):
        return jnp.logical_and(z_ >= 0, z_ < NZ)

    def origins(distance):
        if distance == 0:
            return [(0, zl, None)]
        if not 0 < distance < NZ:
            return []
        return [(sign, lax.rem(zl + sign * distance + 2 * NZ, NZ), in_line(zl + sign * distance)) for sign in (-1, 1)]

    def even(v):
        return lax.rem(v, 2) == 0

    def odd(v):
        return lax.rem(v, 2) == 1

    for sign in (1, -1):
        send(piece_a(zl, y), za_recv.at[zl], z_dev(sign), in_line(zl + sign))
    for y_ in (y_up, y_dn):
        send(piece_a(zl, y), ya_recv.at[zl * NY + y], device(zl, y_, c), None)
    for y_ in (y_up, y_dn):
        send(piece_b(zl, y), yb_recv.at[y], device(zl, y_, c), None)
    send(own_rows, pair_recv, partner, None)
    for stage in range(1, 7):
        for sign, o, there in origins(stage):
            arrived(piece_a(o, y), za_recv.at[o], there)
            send(piece_a(o, y), za_recv.at[o], z_dev(-sign), both(there, in_line(zl - sign)))
            for y_ in (y_up, y_dn):
                send(piece_a(o, y), ya_recv.at[o * NY + y], device(zl, y_, c), there)
            send(piece_a(o, y), pair_recv, partner, there)
        for sign, o, there in origins(stage - 1):
            for y_from, y_to, turn in ((y_dn, y_up, even), (y_up, y_dn, odd)):
                arrived(piece_a(o, y_from), ya_recv.at[o * NY + y_from], there)
                send(piece_a(o, y_from), ya_recv.at[o * NY + y_from], device(zl, y_to, c), both(there, turn(o)))
                send(piece_a(o, y_from), pair_recv, partner, there)
        if stage == 1:
            for y_from, y_to, turn in ((y_dn, y_up, even), (y_up, y_dn, odd)):
                arrived(piece_b(zl, y_from), yb_recv.at[y_from], None)
                send(piece_b(zl, y_from), yb_recv.at[y_from], device(zl, y_to, c), turn(zl))
                send(piece_b(zl, y_from), pair_recv, partner, None)
        if stage >= 2:
            for sign, o, there in origins(stage - 2):
                arrived(piece_a(o, y_far), ya_recv.at[o * NY + y_far], there)
                send(piece_a(o, y_far), pair_recv, partner, there)
        if stage == 2:
            arrived(piece_b(zl, y_far), yb_recv.at[y_far], None)
            send(piece_b(zl, y_far), pair_recv, partner, None)
            for y_ in range(NY):
                for sign in (1, -1):
                    send(piece_b(zl, y_), zb_recv.at[zl * NY + y_], z_dev(sign), in_line(zl + sign))
        for sign, o, there in origins(stage - 3) if stage > 3 else []:
            for y_ in range(NY):
                arrived(piece_b(o, y_), zb_recv.at[o * NY + y_], there)
                send(piece_b(o, y_), zb_recv.at[o * NY + y_], z_dev(-sign), both(there, in_line(zl - sign)))
                send(piece_b(o, y_), pair_recv, partner, there)
    arrived(weight.at[pl.ds(0, D // 2)], pair_recv, None)

    load_hist.wait()

    @pl.when(jnp.logical_not(has_prev))
    def _():
        load_first.wait()

    lane = lax.broadcasted_iota(jnp.int32, (MR, BLOCK), 1)
    gain_row = gain[...]

    def rms(x):
        return lax.rsqrt(jnp.mean(x * x, axis=-1, keepdims=True) + 1e-05)

    def coded(v):
        scale = (jnp.max(jnp.abs(v), axis=-1, keepdims=True) + 1e-06).astype(bf16).astype(f32)
        return (v / scale).astype(bf16).astype(f32) * scale, scale

    def micro_copy(src, dst, rows, cols, send_sem, recv_sem, dev):
        return pltpu.make_async_remote_copy(
            src_ref=src.at[rows, cols], dst_ref=dst.at[rows, cols], send_sem=send_sem, recv_sem=recv_sem,
            device_id=dev, device_id_type=MESH,
        )

    every = pl.ds(0, D)

    def forward(m, _):
        rows = pl.ds(pl.multiple_of(m * MR, MR), MR)

        @pl.when(has_prev)
        def _():
            micro_copy(x_out, x_in, rows, every, f_send.at[m], f_recv.at[m], prev_dev).wait_recv()

        x = x_in[rows, :].astype(f32)
        nrm = (x * rms(x) * gain_row).astype(bf16)
        normed[rows, :] = nrm
        slot = ids[0, m * MR // SEQ]
        prev = hist[slot, pl.ds(pl.multiple_of(lax.rem(m * MR, SEQ), MR), MR), :]
        scale_rows = jnp.zeros((MR, BLOCK), f32)
        for n in range(D // COLS):
            cols = slice(n * COLS, (n + 1) * COLS)
            z = jnp.dot(nrm, weight[:, cols], preferred_element_type=f32)
            sig = 1.0 / (1.0 + jnp.exp(-z))
            factor[rows, cols] = sig * (1.0 + z * (1.0 - sig))
            res = (x[:, cols] + z * sig).astype(bf16)
            out[rows, cols] = res
            old = prev[:, cols].astype(f32)
            delta = res.astype(f32) - old
            for b in range(COLS // BLOCK):
                part = slice(b * BLOCK, (b + 1) * BLOCK)
                decoded, scale = coded(delta[:, part])
                scale_rows = jnp.where(lane == n * (COLS // BLOCK) + b, scale, scale_rows)
                x_out[rows, n * COLS + b * BLOCK : n * COLS + (b + 1) * BLOCK] = (old[:, part] + decoded).astype(bf16)

            @pl.when(has_next)
            def _():
                micro_copy(x_out, x_in, rows, pl.ds(n * COLS, COLS), f_send.at[m], f_recv.at[m], next_dev).start()
        scale_buf[rows, :] = scale_rows.astype(bf16)
        return 0

    lax.fori_loop(0, MICRO, forward, 0)
    scales[...] = scale_buf[:, : D // BLOCK]

    @pl.when(jnp.logical_not(has_next))
    def _():
        load_up.wait()

    gain_acc[...] = jnp.zeros_like(gain_acc)

    def backward(m, _):
        rows = pl.ds(pl.multiple_of(m * MR, MR), MR)

        @pl.when(has_next)
        def _():
            micro_copy(g_out, g_in, rows, every, b_send.at[m], b_recv.at[m], next_dev).wait_recv()

        g = g_in[rows, :].astype(f32)
        dz = (g * factor[rows, :]).astype(bf16)
        dmixed[rows, :] = dz
        x = x_in[rows, :].astype(f32)
        inverse = rms(x)
        unit = x * inverse
        dn = lax.dot_general(dz, weight[...], (((1,), (1,)), ((), ())), preferred_element_type=f32)

        @pl.when(has_prev)
        def _():
            du = dn * gain_row
            shared = jnp.mean(du * unit, axis=-1, keepdims=True)
            dx = g + inverse * (du - unit * shared)
            for n in range(D // COLS):
                for b in range(COLS // BLOCK):
                    part = slice(n * COLS + b * BLOCK, n * COLS + (b + 1) * BLOCK)
                    decoded, _ = coded(dx[:, part])
                    g_out[rows, part] = decoded.astype(bf16)
                micro_copy(g_out, g_in, rows, pl.ds(n * COLS, COLS), b_send.at[m], b_recv.at[m], prev_dev).start()

        prod = dn * unit
        total = prod[0:8]
        for k in range(1, MR // 8):
            total = total + prod[8 * k : 8 * k + 8]
        gain_acc[...] += total
        return 0

    lax.fori_loop(0, MICRO, backward, 0)
    gain_out[...] = jnp.sum(gain_acc[...], axis=0, keepdims=True)

    def drain(m, _):
        rows = pl.ds(pl.multiple_of(m * MR, MR), MR)

        @pl.when(has_next)
        def _():
            micro_copy(x_out, x_in, rows, every, f_send.at[m], f_recv.at[m], next_dev).wait_send()

        @pl.when(has_prev)
        def _():
            micro_copy(g_out, g_in, rows, every, b_send.at[m], b_recv.at[m], prev_dev).wait_send()

        return 0

    lax.fori_loop(0, MICRO, drain, 0)
    for copy, cond in sends:
        if cond is None:
            copy.wait_send()
        else:
            pl.when(cond)(copy.wait_send)


def body(first_input, upstream, history, example_ids, norm_gain, weight):
    vmem = pl.BlockSpec(memory_space=pltpu.VMEM)
    anywhere = pl.BlockSpec(memory_space=pl.ANY)
    smem = pl.BlockSpec(memory_space=pltpu.SMEM)
    dma = pltpu.SemaphoreType.DMA
    out, scales, normed, dmixed, gain_part = pl.pallas_call(
        relay_kernel,
        out_shape=(
            jax.ShapeDtypeStruct((TOK, D), bf16),
            jax.ShapeDtypeStruct((TOK, D // BLOCK), bf16),
            jax.ShapeDtypeStruct((TOK, D), bf16),
            jax.ShapeDtypeStruct((TOK, D), bf16),
            jax.ShapeDtypeStruct((1, D), f32),
        ),
        in_specs=[anywhere, anywhere, anywhere, smem, vmem, anywhere],
        out_specs=(vmem,) * 5,
        scratch_shapes=[
            pltpu.VMEM((D, D), bf16),
            pltpu.VMEM((4, SEQ, D), bf16),
            pltpu.VMEM((TOK, D), bf16),
            pltpu.VMEM((TOK, D), bf16),
            pltpu.VMEM((TOK, D), bf16),
            pltpu.VMEM((TOK, D), bf16),
            pltpu.VMEM((TOK, D), f32),
            pltpu.VMEM((TOK, BLOCK), bf16),
            pltpu.VMEM((8, D), f32),
            dma((4,)),
            dma((MICRO,)), dma((MICRO,)), dma((MICRO,)), dma((MICRO,)),
            dma((NZ,)), dma((NZ * NY,)), dma((NY,)), dma((NZ * NY,)), dma(()), dma((136,)),
        ],
        compiler_params=pltpu.CompilerParams(
            collective_id=0, has_side_effects=True, vmem_limit_bytes=48 * 2**20
        ),
    )(first_input, upstream, history, example_ids, norm_gain, weight)
    weight_grad = lax.psum_scatter(
        lax.dot_general(
            normed, dmixed, (((0,), (0,)), ((), ())), preferred_element_type=f32
        ).astype(bf16),
        "dp", scatter_dimension=0, tiled=True,
    ).astype(f32)
    gain_grad = lax.psum(gain_part, "dp")
    return (out[None], scales[None], weight_grad[None], gain_grad)


def solution(mesh):
    return jax.shard_map(
        body,
        mesh=mesh,
        in_specs=(
            P("dp", None),
            P("dp", None),
            P("section", None, "dp", None, None),
            P("dp", None),
            P("section", None),
            P("section", "dp", None),
        ),
        out_specs=(
            P("section", "dp", None),
            P("section", "dp", None),
            P("section", "dp", None),
            P("section", None),
        ),
        check_vma=False,
    )
```

```python
import functools

import jax
import jax.numpy as jnp
from jax import lax
from jax.experimental import pallas as pl
from jax.experimental.pallas import tpu as pltpu
from jax.sharding import PartitionSpec as P

MESH = pl.DeviceIdType.MESH
D = 2048
TOK = 256
SEQ = 64
BLOCK = 128
N_SECTION = 8
NZ = 4
NY = 4
SHARD = 64
ROWS_A = 48
ROWS_B = SHARD - ROWS_A
MICRO = 8
MR = TOK // MICRO
WIDE = 64
HALF = D // 2
LAST = N_SECTION - 1
NEAR, OVER = 3, 4
COLS = 512
bf16 = jnp.bfloat16
f32 = jnp.float32


def relay_kernel(
    first_hbm, up_hbm, hist_hbm, ids, gain, w_hbm,
    out, scales, weight_grad, gain_out,
    weight, weight_t, hist, x_in, g_in, x_out, g_out, f_relay, b_relay, factor, normed, scale_buf, gain_acc, gain_buf,
    pack, pack_out, dmixed, part_a, part_b, y_far_in, y_in, z_in, zb_in, yb_far_in, yb_in,
    local_sem, f_send, f_recv, b_send, b_recv, rf_send, rf_recv, rb_send, rb_recv,
    za_recv, ya_recv, yb_recv, zb_recv, pair_recv, ag_send,
    pack_sems, dz_send, dz_recv, gain_send, gain_recv,
    rs_send, far_recv, ring_recv, line_recv, lineb_recv, farb_recv, ringb_recv,
):
    dp = lax.axis_index("dp")
    s = lax.axis_index("section")
    zl = dp // 8
    y = lax.rem(dp // 2, NY)
    c = lax.rem(dp, 2)

    def device(zl_, y_, c_):
        return (zl_ * 8 + y_ * 2 + c_, s)

    def at_section(s_):
        return (dp, s_)

    y_up, y_dn, y_far = lax.rem(y + 1, NY), lax.rem(y + 3, NY), lax.rem(y + 2, NY)
    partner = device(zl, y, 1 - c)
    prev_dev, next_dev = at_section(lax.rem(s + 7, 8)), at_section(lax.rem(s + 1, 8))
    is_first, is_last = s == 0, s == LAST
    has_prev, has_next = s > 0, s < LAST
    direct_prev = jnp.logical_and(has_prev, s != OVER)
    direct_next = jnp.logical_and(has_next, s != NEAR)

    def z_dev(step):
        return device(lax.rem(zl + step + NZ, NZ), y, c)

    def row_of(zl_, y_, c_):
        return pl.multiple_of(((zl_ * NY + y_) * 2 + c_) * SHARD, SHARD)

    own_rows = weight.at[pl.ds(row_of(zl, y, c), SHARD)]
    load_w = pltpu.make_async_copy(w_hbm.at[0], own_rows, local_sem.at[0])
    load_w.start()
    load_hist = pltpu.make_async_copy(hist_hbm.at[0, 0], hist, local_sem.at[1])
    load_hist.start()
    load_first = pltpu.make_async_copy(first_hbm, x_in, local_sem.at[2])
    load_up = pltpu.make_async_copy(up_hbm, g_in, local_sem.at[3])
    pl.when(is_first)(load_first.start)
    pl.when(is_last)(load_up.start)

    barrier = pltpu.get_barrier_semaphore()
    z_skip = device(lax.rem(zl + 2, NZ), y, c)
    for dev in (partner, device(zl, y_up, c), device(zl, y_dn, c), device(zl, y_far, c), z_skip):
        pl.semaphore_signal(barrier, inc=1, device_id=dev, device_id_type=MESH)
    ends = jnp.logical_or(is_first, is_last)
    middle = jnp.logical_or(s == NEAR, s == OVER)
    others = (
        (z_dev(-1), zl > 0), (z_dev(1), zl < NZ - 1), (prev_dev, direct_prev), (next_dev, direct_next),
        (at_section(NEAR), ends), (at_section(OVER), ends), (at_section(0), middle), (at_section(LAST), middle),
    )
    greeted = jnp.int32(5)
    for dev, there in others:
        greeted = greeted + there.astype(jnp.int32)

        @pl.when(there)
        def _():
            pl.semaphore_signal(barrier, inc=1, device_id=dev, device_id_type=MESH)

    pl.semaphore_wait(barrier, greeted)
    load_w.wait()

    sends = []

    def piece_a(zl_, y_):
        return weight.at[pl.ds(row_of(zl_, y_, c), ROWS_A)]

    def piece_b(zl_, y_):
        return weight.at[pl.ds(pl.multiple_of(row_of(zl_, y_, c) + ROWS_A, 16), SHARD - ROWS_A)]

    def send(ref, recv_sem, dev, cond):
        copy = pltpu.make_async_remote_copy(
            src_ref=ref, dst_ref=ref, send_sem=ag_send.at[len(sends)], recv_sem=recv_sem,
            device_id=dev, device_id_type=MESH,
        )
        sends.append((copy, cond))
        if cond is None:
            copy.start()
        else:
            pl.when(cond)(copy.start)

    def arrived(ref, recv_sem, cond):
        copy = pltpu.make_async_remote_copy(
            src_ref=ref, dst_ref=ref, send_sem=ag_send.at[0], recv_sem=recv_sem,
            device_id=partner, device_id_type=MESH,
        )
        if cond is None:
            copy.wait_recv()
        else:
            pl.when(cond)(copy.wait_recv)

    def both(a, b):
        return b if a is None else jnp.logical_and(a, b)

    def in_line(z_):
        return jnp.logical_and(z_ >= 0, z_ < NZ)

    def origins(distance):
        if distance == 0:
            return [(0, zl, None)]
        if not 0 < distance < NZ:
            return []
        return [(sign, lax.rem(zl + sign * distance + 2 * NZ, NZ), in_line(zl + sign * distance)) for sign in (-1, 1)]

    def even(v):
        return lax.rem(v, 2) == 0

    def odd(v):
        return lax.rem(v, 2) == 1

    for sign in (1, -1):
        send(piece_a(zl, y), za_recv.at[zl], z_dev(sign), in_line(zl + sign))
    for y_ in (y_up, y_dn):
        send(piece_a(zl, y), ya_recv.at[zl * NY + y], device(zl, y_, c), None)
    for y_ in (y_up, y_dn):
        send(piece_b(zl, y), yb_recv.at[y], device(zl, y_, c), None)
    send(own_rows, pair_recv, partner, None)
    for stage in range(1, 7):
        for sign, o, there in origins(stage):
            arrived(piece_a(o, y), za_recv.at[o], there)
            send(piece_a(o, y), za_recv.at[o], z_dev(-sign), both(there, in_line(zl - sign)))
            for y_ in (y_up, y_dn):
                send(piece_a(o, y), ya_recv.at[o * NY + y], device(zl, y_, c), there)
            send(piece_a(o, y), pair_recv, partner, there)
        for sign, o, there in origins(stage - 1):
            for y_from, y_to, turn in ((y_dn, y_up, even), (y_up, y_dn, odd)):
                arrived(piece_a(o, y_from), ya_recv.at[o * NY + y_from], there)
                send(piece_a(o, y_from), ya_recv.at[o * NY + y_from], device(zl, y_to, c), both(there, turn(o)))
                send(piece_a(o, y_from), pair_recv, partner, there)
        if stage == 1:
            for y_from, y_to, turn in ((y_dn, y_up, even), (y_up, y_dn, odd)):
                arrived(piece_b(zl, y_from), yb_recv.at[y_from], None)
                send(piece_b(zl, y_from), yb_recv.at[y_from], device(zl, y_to, c), turn(zl))
                send(piece_b(zl, y_from), pair_recv, partner, None)
        if stage >= 2:
            for sign, o, there in origins(stage - 2):
                arrived(piece_a(o, y_far), ya_recv.at[o * NY + y_far], there)
                send(piece_a(o, y_far), pair_recv, partner, there)
        if stage == 2:
            arrived(piece_b(zl, y_far), yb_recv.at[y_far], None)
            send(piece_b(zl, y_far), pair_recv, partner, None)
            for y_ in range(NY):
                for sign in (1, -1):
                    send(piece_b(zl, y_), zb_recv.at[zl * NY + y_], z_dev(sign), in_line(zl + sign))
        for sign, o, there in origins(stage - 3) if stage > 3 else []:
            for y_ in range(NY):
                arrived(piece_b(o, y_), zb_recv.at[o * NY + y_], there)
                send(piece_b(o, y_), zb_recv.at[o * NY + y_], z_dev(-sign), both(there, in_line(zl - sign)))
                send(piece_b(o, y_), pair_recv, partner, there)
    arrived(weight.at[pl.ds(0, D // 2)], pair_recv, None)

    load_hist.wait()
    pl.when(is_first)(load_first.wait)
    pl.when(is_last)(load_up.wait)
    gain_acc[...] = jnp.zeros_like(gain_acc)

    def remote(src_ref, dst_ref, send_sem, recv_sem, dev):
        return pltpu.make_async_remote_copy(
            src_ref=src_ref, dst_ref=dst_ref, send_sem=send_sem, recv_sem=recv_sem,
            device_id=dev, device_id_type=MESH,
        )

    def rms(x):
        return lax.rsqrt(jnp.mean(x * x, axis=-1, keepdims=True) + 1e-05)

    def coded(v):
        scale = (jnp.max(jnp.abs(v), axis=-1, keepdims=True) + 1e-06).astype(bf16).astype(f32)
        return (v * (1.0 / scale)).astype(bf16).astype(f32) * scale, scale

    def rows_at(m):
        return pl.ds(pl.multiple_of(m * MR, MR), MR)

    every, low, high = pl.ds(0, D), pl.ds(0, HALF), pl.ds(HALF, HALF)

    def forward_rows(m, size, sending):
        rows = pl.ds(pl.multiple_of(m * MR, MR), size)

        @pl.when(has_prev)
        def _():
            for k in range(size // MR):
                part = rows_at(m + k)
                remote(x_out.at[part], x_in.at[part], f_send.at[m + k], f_recv.at[m + k], prev_dev).wait_recv()

        x = x_in[rows, :].astype(f32)
        nrm = (x * rms(x) * gain[...]).astype(bf16)
        normed[rows, :] = nrm
        slot = ids[0, m * MR // SEQ]
        old_rows = pl.ds(pl.multiple_of(lax.rem(m * MR, SEQ), MR), size)
        lane = lax.broadcasted_iota(jnp.int32, (size, BLOCK), 1)
        scale_rows = jnp.zeros((size, BLOCK), f32)
        for n in range(D // COLS):
            cols = slice(n * COLS, (n + 1) * COLS)
            z = jnp.dot(nrm, weight[:, cols], preferred_element_type=f32)
            sig = 0.5 + 0.5 * jnp.tanh(0.5 * z)
            factor[rows, cols] = sig * (1.0 + z * (1.0 - sig))
            res = (x_in[rows, cols].astype(f32) + z * sig).astype(bf16)
            out[rows, cols] = res
            old = hist[slot, old_rows, cols].astype(f32)
            delta = res.astype(f32) - old
            for b in range(COLS // BLOCK):
                part = slice(b * BLOCK, (b + 1) * BLOCK)
                decoded, scale = coded(delta[:, part])
                scale_rows = jnp.where(lane == n * (COLS // BLOCK) + b, scale, scale_rows)
                if sending:
                    x_out[rows, n * COLS + b * BLOCK : n * COLS + (b + 1) * BLOCK] = (old[:, part] + decoded).astype(bf16)
            if sending:
                here = pl.ds(n * COLS, COLS)
                there = pl.ds(n * COLS % HALF, COLS)
                via = 0 if n * COLS < HALF else LAST
                direct = remote(x_out.at[rows, here], x_in.at[rows, here], f_send.at[m], f_recv.at[m], next_dev)
                hop = remote(x_out.at[rows, here], f_relay.at[rows, there], f_send.at[m], rf_recv.at[m], at_section(via))
                pl.when(direct_next)(direct.start)
                pl.when(s == NEAR)(hop.start)
        scale_buf[rows, :] = scale_rows.astype(bf16)

    def backward_rows(m, size):
        rows = pl.ds(pl.multiple_of(m * MR, MR), size)

        @pl.when(has_next)
        def _():
            for k in range(size // MR):
                part = rows_at(m + k)
                remote(g_out.at[part], g_in.at[part], b_send.at[m + k], b_recv.at[m + k], next_dev).wait_recv()

        g = g_in[rows, :].astype(f32)
        dz = (g * factor[rows, :]).astype(bf16)
        dmixed[rows, :] = dz
        for k in range(size // MR):
            dz_copy(m + k).start()
        x = x_in[rows, :].astype(f32)
        inverse = rms(x)
        unit = x * inverse
        dn = jnp.dot(dz, weight_t[...], preferred_element_type=f32)

        @pl.when(has_prev)
        def _():
            du = dn * gain[...]
            shared = jnp.mean(du * unit, axis=-1, keepdims=True)
            dx = g + inverse * (du - unit * shared)
            for n in range(D // COLS):
                for b in range(COLS // BLOCK):
                    part = slice(n * COLS + b * BLOCK, n * COLS + (b + 1) * BLOCK)
                    decoded, _ = coded(dx[:, part])
                    g_out[rows, part] = decoded.astype(bf16)
                here = pl.ds(n * COLS, COLS)
                there = pl.ds(n * COLS % HALF, COLS)
                via = 0 if n * COLS < HALF else LAST
                for k in range(size // MR):
                    sub = rows_at(m + k)
                    direct = remote(g_out.at[sub, here], g_in.at[sub, here], b_send.at[m + k], b_recv.at[m + k], prev_dev)
                    pl.when(direct_prev)(direct.start)
                    if size == MR:
                        hop = remote(g_out.at[sub, here], b_relay.at[sub, there], b_send.at[m + k], rb_recv.at[m + k], at_section(via))
                        pl.when(s == OVER)(hop.start)

        prod = dn * unit
        total = prod[0:8]
        for k in range(1, size // 8):
            total = total + prod[8 * k : 8 * k + 8]
        gain_acc[...] += total

    def dz_copy(m):
        here = rows_at(m)
        there = pl.ds(pl.multiple_of(TOK + m * MR, MR), MR)
        return remote(dmixed.at[here], dmixed.at[there], dz_send.at[m], dz_recv.at[m], partner)

    def relay_forward(m, _):
        rows = rows_at(m)

        def passed(cols):
            return remote(f_relay.at[rows], x_in.at[rows, cols], rf_send.at[m], f_recv.at[m], at_section(OVER))

        remote(f_relay.at[rows], f_relay.at[rows], rf_send.at[m], rf_recv.at[m], at_section(NEAR)).wait_recv()
        pl.when(is_first)(passed(low).start)
        pl.when(is_last)(passed(high).start)
        return 0

    def relay_backward(m, _):
        rows = rows_at(m)

        def passed(cols):
            return remote(b_relay.at[rows], g_in.at[rows, cols], rb_send.at[m], b_recv.at[m], at_section(NEAR))

        remote(b_relay.at[rows], b_relay.at[rows], rb_send.at[m], rb_recv.at[m], at_section(OVER)).wait_recv()
        pl.when(is_first)(passed(low).start)
        pl.when(is_last)(passed(high).start)
        return 0

    def transpose_weight(i, _):
        rows = pl.ds(pl.multiple_of(i * 256, 256), 256)
        for j in range(D // 256):
            weight_t[j * 256 : (j + 1) * 256, rows] = weight[rows, j * 256 : (j + 1) * 256].T
        return 0

    def pack_normed(m, _):
        rows = rows_at(m)
        lane = lax.broadcasted_iota(jnp.int32, (MR, BLOCK), 1)
        for t in range(D // 256):
            a = normed[rows, 256 * t : 256 * t + 128].astype(f32)
            b = normed[rows, 256 * t + 128 : 256 * t + 256].astype(f32)
            zero = jnp.where(lane < SHARD, a, pltpu.roll(b, SHARD, 1))
            one = jnp.where(lane < SHARD, pltpu.roll(a, SHARD, 1), b)
            pack[rows, 128 * t : 128 * t + 128] = jnp.where(c == 0, zero, one).astype(bf16)
            pack_out[rows, 128 * t : 128 * t + 128] = jnp.where(c == 0, one, zero).astype(bf16)
        return 0

    pack_copy = remote(pack_out, pack.at[pl.ds(TOK, TOK)], pack_sems.at[0], pack_sems.at[1], partner)

    def forward_step(m, _):
        forward_rows(m, MR, True)
        return 0

    def backward_step(m, _):
        backward_rows(m, MR)
        return 0

    def turn_step(i, _):
        forward_rows(i * (WIDE // MR), WIDE, False)
        backward_rows(i * (WIDE // MR), WIDE)
        return 0

    @pl.when(s >= OVER)
    def _():
        lax.fori_loop(0, D // 256, transpose_weight, 0)

    @pl.when(is_last)
    def _():
        lax.fori_loop(0, MICRO, relay_forward, 0)
        lax.fori_loop(0, TOK // WIDE, turn_step, 0)
        lax.fori_loop(0, MICRO, relay_backward, 0)

    @pl.when(has_next)
    def _():
        lax.fori_loop(0, MICRO, forward_step, 0)

        @pl.when(is_first)
        def _():
            lax.fori_loop(0, MICRO, relay_forward, 0)

        @pl.when(s < OVER)
        def _():
            lax.fori_loop(0, D // 256, transpose_weight, 0)
            lax.fori_loop(0, MICRO, pack_normed, 0)
            pack_copy.start()

        @pl.when(is_first)
        def _():
            lax.fori_loop(0, MICRO, relay_backward, 0)

        lax.fori_loop(0, MICRO, backward_step, 0)

    @pl.when(s >= OVER)
    def _():
        lax.fori_loop(0, MICRO, pack_normed, 0)
        pack_copy.start()

    pack_copy.wait_recv()
    for m in range(MICRO):
        dz_copy(m).wait_recv()
    scatter = []

    def hand(src_ref, dst_ref, recv_sem, dev, cond=None):
        copy = remote(src_ref, dst_ref, rs_send.at[len(scatter)], recv_sem, dev)
        scatter.append((copy, cond))
        if cond is None:
            copy.start()
        else:
            pl.when(cond)(copy.start)

    def landed(ref, recv_sem, cond=None):
        copy = remote(ref, ref, rs_send.at[0], recv_sem, partner)
        if cond is None:
            copy.wait_recv()
        else:
            pl.when(cond)(copy.wait_recv)

    def add_to(ref, *terms):
        total = ref[...].astype(f32)
        for term in terms:
            total = total + term[...].astype(f32)
        ref[...] = total.astype(ref.dtype)

    low_half = zl < 2
    order = (
        jnp.where(low_half, 3, 0), jnp.where(low_half, 2, 1), jnp.where(low_half, 1 - zl, 5 - zl), zl,
    )
    up_dev, dn_dev = device(zl, y_up, c), device(zl, y_dn, c)

    def line(k):
        right = order[k] > zl
        upstream = jnp.where(right, zl > 0, zl < NZ - 1)
        return right, upstream, jnp.where(right, 0, 1)

    def send_line_b(k, cond):
        right, _, side = line(k)
        zd = order[k]
        for step, way in ((1, right), (-1, jnp.logical_not(right))):
            hand(part_b.at[zd], zb_in.at[side, zd], lineb_recv.at[side * NZ + zd], z_dev(step), both(cond, way))

    def send_line_a(k, cond):
        right, _, side = line(k)
        zd = order[k]
        for step, way in ((1, right), (-1, jnp.logical_not(right))):
            hand(part_a.at[zd, y], z_in.at[side, zd], line_recv.at[side * NZ + zd], z_dev(step), both(cond, way))

    def pass_line_b(k):
        _, upstream, side = line(k)
        zd = order[k]
        landed(zb_in.at[side, zd], lineb_recv.at[side * NZ + zd], upstream)

        @pl.when(upstream)
        def _():
            add_to(part_b.at[zd], zb_in.at[side, zd])

        send_line_b(k, upstream)

    def pass_line_a(k):
        _, upstream, side = line(k)
        zd = order[k]
        landed(z_in.at[side, zd], line_recv.at[side * NZ + zd], upstream)

        @pl.when(upstream)
        def _():
            add_to(part_a.at[zd, y], z_in.at[side, zd])

        send_line_a(k, upstream)

    def ring_out(k):
        zd = order[k]
        landed(y_far_in.at[zd], far_recv.at[zd])
        target = jnp.where(even(zd), y_up, y_dn)
        add_to(part_a.at[zd, target], y_far_in.at[zd])
        hand(part_a.at[zd, y_up], y_in.at[zd, 0], ring_recv.at[zd * 2], up_dev)
        hand(part_a.at[zd, y_dn], y_in.at[zd, 1], ring_recv.at[zd * 2 + 1], dn_dev)

    def ring_in(k):
        zd = order[k]
        for side in range(2):
            landed(y_in.at[zd, side], ring_recv.at[zd * 2 + side])
        if k < NZ - 1:
            add_to(part_a.at[zd, y], y_in.at[zd, 0], y_in.at[zd, 1])
            send_line_a(k, jnp.logical_not(line(k)[1]))
        else:
            weight_grad[0:ROWS_A, :] = (
                part_a[zd, y].astype(f32) + y_in[zd, 0].astype(f32) + y_in[zd, 1].astype(f32)
            )

    gain_steps = (
        partner, device(zl, jnp.where(even(y), y + 1, y - 1), c), device(zl, y_far, c),
        device(jnp.where(even(zl), zl + 1, zl - 1), y, c), z_skip,
    )
    gain_buf[0] = jnp.sum(gain_acc[...], axis=0, keepdims=True)

    def gain_copy(k):
        return remote(gain_buf.at[k], gain_buf.at[6 + k], gain_send.at[k], gain_recv.at[k], gain_steps[k])

    def gain_add(k):
        gain_copy(k).wait_recv()
        gain_buf[k + 1] = gain_buf[k] + gain_buf[6 + k]
        if k + 1 < len(gain_steps):
            gain_copy(k + 1).start()

    for k in range(NZ):
        zd = order[k]
        cols = pl.ds(pl.multiple_of(zd * 256, 256), 256)
        total = lax.dot_general(pack[:, cols], dmixed[...], (((0,), (0,)), ((), ())), preferred_element_type=f32).astype(bf16)
        for j in range(NY):
            part_a[zd, j] = total[j * SHARD : j * SHARD + ROWS_A]
            part_b[zd, j * ROWS_B : (j + 1) * ROWS_B] = total[j * SHARD + ROWS_A : (j + 1) * SHARD]
        for dev, way in ((up_dev, even(zd)), (dn_dev, odd(zd))):
            hand(part_a.at[zd, y_far], y_far_in.at[zd], far_recv.at[zd], dev, way)
        if k < NZ - 1:
            send_line_b(k, jnp.logical_not(line(k)[1]))
        if k == 0:
            gain_copy(0).start()
    ring_out(0)
    ring_out(1)
    gain_add(0)
    pass_line_b(0)
    ring_out(2)
    ring_out(3)
    gain_add(1)
    ring_in(0)
    pass_line_b(1)
    gain_add(2)
    ring_in(1)
    pass_line_b(2)
    gain_add(3)

    def own_line(slot, sems):
        for side, there in ((0, zl > 0), (1, zl < NZ - 1)):
            landed(slot(side), sems.at[side * NZ + zl], there)

    own_line(lambda side: zb_in.at[side, zl], lineb_recv)
    for side, there in ((0, zl > 0), (1, zl < NZ - 1)):
        @pl.when(there)
        def _():
            add_to(part_b.at[zl], zb_in.at[side, zl])

    def b_rows(y_):
        return pl.ds(pl.multiple_of(y_ * ROWS_B, ROWS_B), ROWS_B)

    for dev, way in ((up_dev, even(zl)), (dn_dev, odd(zl))):
        hand(part_b.at[zl, b_rows(y_far)], yb_far_in, farb_recv, dev, way)
    ring_in(2)
    gain_add(4)
    landed(yb_far_in, farb_recv)
    add_to(part_b.at[zl, b_rows(jnp.where(even(zl), y_up, y_dn))], yb_far_in)
    hand(part_b.at[zl, b_rows(y_up)], yb_in.at[0], ringb_recv.at[0], up_dev)
    hand(part_b.at[zl, b_rows(y_dn)], yb_in.at[1], ringb_recv.at[1], dn_dev)
    for k in range(NZ - 1):
        pass_line_a(k)
    ring_in(3)
    for side in range(2):
        landed(yb_in.at[side], ringb_recv.at[side])
    weight_grad[ROWS_A:SHARD, :] = (
        part_b[zl, b_rows(y)].astype(f32) + yb_in[0].astype(f32) + yb_in[1].astype(f32)
    )
    own_line(lambda side: z_in.at[side, zl], line_recv)
    for side, there in ((0, zl > 0), (1, zl < NZ - 1)):
        @pl.when(there)
        def _():
            weight_grad[0:ROWS_A, :] += z_in[side, zl].astype(f32)

    gain_out[...] = gain_buf[5]
    scales[...] = scale_buf[:, : D // BLOCK]

    def drain(m, _):
        rows = rows_at(m)
        dz_copy(m).wait_send()

        @pl.when(has_next)
        def _():
            remote(x_out.at[rows], x_in.at[rows], f_send.at[m], f_recv.at[m], next_dev).wait_send()

        @pl.when(has_prev)
        def _():
            remote(g_out.at[rows], g_in.at[rows], b_send.at[m], b_recv.at[m], prev_dev).wait_send()

        @pl.when(ends)
        def _():
            remote(f_relay.at[rows], f_relay.at[rows], rf_send.at[m], rf_recv.at[m], at_section(OVER)).wait_send()
            remote(b_relay.at[rows], b_relay.at[rows], rb_send.at[m], rb_recv.at[m], at_section(NEAR)).wait_send()

        return 0

    lax.fori_loop(0, MICRO, drain, 0)
    pack_copy.wait_send()
    for k in range(len(gain_steps)):
        gain_copy(k).wait_send()
    for copy, cond in sends + scatter:
        if cond is None:
            copy.wait_send()
        else:
            pl.when(cond)(copy.wait_send)


def body(first_input, upstream, history, example_ids, norm_gain, weight):
    vmem = pl.BlockSpec(memory_space=pltpu.VMEM)
    anywhere = pl.BlockSpec(memory_space=pl.ANY)
    smem = pl.BlockSpec(memory_space=pltpu.SMEM)
    dma = pltpu.SemaphoreType.DMA
    out, scales, weight_grad, gain_grad = pl.pallas_call(
        relay_kernel,
        out_shape=(
            jax.ShapeDtypeStruct((TOK, D), bf16),
            jax.ShapeDtypeStruct((TOK, D // BLOCK), bf16),
            jax.ShapeDtypeStruct((SHARD, D), f32),
            jax.ShapeDtypeStruct((1, D), f32),
        ),
        in_specs=[anywhere, anywhere, anywhere, smem, vmem, anywhere],
        out_specs=(vmem,) * 4,
        scratch_shapes=[
            pltpu.VMEM((D, D), bf16),
            pltpu.VMEM((D, D), bf16),
            pltpu.VMEM((4, SEQ, D), bf16),
            pltpu.VMEM((TOK, D), bf16),
            pltpu.VMEM((TOK, D), bf16),
            pltpu.VMEM((TOK, D), bf16),
            pltpu.VMEM((TOK, D), bf16),
            pltpu.VMEM((TOK, HALF), bf16),
            pltpu.VMEM((TOK, HALF), bf16),
            pltpu.VMEM((TOK, D), f32),
            pltpu.VMEM((TOK, D), bf16),
            pltpu.VMEM((TOK, BLOCK), bf16),
            pltpu.VMEM((8, D), f32),
            pltpu.VMEM((11, 1, D), f32),
            pltpu.VMEM((2 * TOK, HALF), bf16),
            pltpu.VMEM((TOK, HALF), bf16),
            pltpu.VMEM((2 * TOK, D), bf16),
            pltpu.VMEM((NZ, NY, ROWS_A, D), bf16),
            pltpu.VMEM((NZ, NY * ROWS_B, D), bf16),
            pltpu.VMEM((NZ, ROWS_A, D), bf16),
            pltpu.VMEM((NZ, 2, ROWS_A, D), bf16),
            pltpu.VMEM((2, NZ, ROWS_A, D), bf16),
            pltpu.VMEM((2, NZ, NY * ROWS_B, D), bf16),
            pltpu.VMEM((ROWS_B, D), bf16),
            pltpu.VMEM((2, ROWS_B, D), bf16),
            dma((4,)),
            dma((MICRO,)), dma((MICRO,)), dma((MICRO,)), dma((MICRO,)),
            dma((MICRO,)), dma((MICRO,)), dma((MICRO,)), dma((MICRO,)),
            dma((NZ,)), dma((NZ * NY,)), dma((NY,)), dma((NZ * NY,)), dma(()), dma((136,)),
            dma((2,)), dma((MICRO,)), dma((MICRO,)), dma((5,)), dma((5,)),
            dma((64,)), dma((NZ,)), dma((NZ * 2,)), dma((2 * NZ,)), dma((2 * NZ,)), dma(()), dma((2,)),
        ],
        compiler_params=pltpu.CompilerParams(
            collective_id=0, has_side_effects=True, vmem_limit_bytes=56 * 2**20
        ),
    )(first_input, upstream, history, example_ids, norm_gain, weight)
    return (out[None], scales[None], weight_grad[None], gain_grad)


def solution(mesh):
    return jax.shard_map(
        body,
        mesh=mesh,
        in_specs=(
            P("dp", None),
            P("dp", None),
            P("section", None, "dp", None, None),
            P("dp", None),
            P("section", None),
            P("section", "dp", None),
        ),
        out_specs=(
            P("section", "dp", None),
            P("section", "dp", None),
            P("section", "dp", None),
            P("section", None),
        ),
        check_vma=False,
    )
```

```python
import functools

import jax
import jax.numpy as jnp
from jax import lax
from jax.experimental import pallas as pl
from jax.experimental.pallas import tpu as pltpu
from jax.sharding import PartitionSpec as P

MESH = pl.DeviceIdType.MESH
D = 2048
TOK = 256
SEQ = 64
BLOCK = 128
N_SECTION = 8
NZ = 4
NY = 4
SHARD = 64
ROWS_A = 48
ROWS_B = SHARD - ROWS_A
MICRO = 16
MR = TOK // MICRO
WIDE = 64
HALF = D // 2
LAST = N_SECTION - 1
NEAR, OVER = 3, 4
COLS = 2048
bf16 = jnp.bfloat16
f32 = jnp.float32


def relay_kernel(
    first_hbm, up_hbm, hist_hbm, ids, gain, w_hbm,
    out, scales, weight_grad, gain_out,
    weight, weight_t, hist, x_in, g_in, x_out, g_out, f_relay, b_relay, factor, normed, inv_buf, du_buf, scale_buf, gain_acc, gain_buf,
    pack, pack_out, dmixed, part_a, part_b, y_far_in, y_in, z_in, zb_in, yb_far_in, yb_in,
    local_sem, f_send, f_recv, b_send, b_recv, rf_send, rf_recv, rb_send, rb_recv,
    za_recv, ya_recv, yb_recv, zb_recv, pair_recv, ag_send,
    pack_sems, dz_send, dz_recv, gain_send, gain_recv,
    rs_send, far_recv, ring_recv, line_recv, lineb_recv, farb_recv, ringb_recv,
):
    dp = lax.axis_index("dp")
    s = lax.axis_index("section")
    zl = dp // 8
    y = lax.rem(dp // 2, NY)
    c = lax.rem(dp, 2)

    def device(zl_, y_, c_):
        return (zl_ * 8 + y_ * 2 + c_, s)

    def at_section(s_):
        return (dp, s_)

    y_up, y_dn, y_far = lax.rem(y + 1, NY), lax.rem(y + 3, NY), lax.rem(y + 2, NY)
    partner = device(zl, y, 1 - c)
    prev_dev, next_dev = at_section(lax.rem(s + 7, 8)), at_section(lax.rem(s + 1, 8))
    is_first, is_last = s == 0, s == LAST
    has_prev, has_next = s > 0, s < LAST
    direct_prev = jnp.logical_and(has_prev, s != OVER)
    direct_next = jnp.logical_and(has_next, s != NEAR)

    def z_dev(step):
        return device(lax.rem(zl + step + NZ, NZ), y, c)

    def row_of(zl_, y_, c_):
        return pl.multiple_of(((zl_ * NY + y_) * 2 + c_) * SHARD, SHARD)

    own_rows = weight.at[pl.ds(row_of(zl, y, c), SHARD)]
    load_w = pltpu.make_async_copy(w_hbm.at[0], own_rows, local_sem.at[0])
    load_w.start()
    load_hist = pltpu.make_async_copy(hist_hbm.at[0, 0], hist, local_sem.at[1])
    load_hist.start()
    load_first = pltpu.make_async_copy(first_hbm, x_in, local_sem.at[2])
    load_up = pltpu.make_async_copy(up_hbm, g_in, local_sem.at[3])
    pl.when(is_first)(load_first.start)
    pl.when(is_last)(load_up.start)

    barrier = pltpu.get_barrier_semaphore()
    z_skip = device(lax.rem(zl + 2, NZ), y, c)
    for dev in (partner, device(zl, y_up, c), device(zl, y_dn, c), device(zl, y_far, c), z_skip):
        pl.semaphore_signal(barrier, inc=1, device_id=dev, device_id_type=MESH)
    ends = jnp.logical_or(is_first, is_last)
    middle = jnp.logical_or(s == NEAR, s == OVER)
    others = (
        (z_dev(-1), zl > 0), (z_dev(1), zl < NZ - 1), (prev_dev, direct_prev), (next_dev, direct_next),
        (at_section(NEAR), ends), (at_section(OVER), ends), (at_section(0), middle), (at_section(LAST), middle),
    )
    greeted = jnp.int32(5)
    for dev, there in others:
        greeted = greeted + there.astype(jnp.int32)

        @pl.when(there)
        def _():
            pl.semaphore_signal(barrier, inc=1, device_id=dev, device_id_type=MESH)

    pl.semaphore_wait(barrier, greeted)
    load_w.wait()

    sends = []

    def piece_a(zl_, y_):
        return weight.at[pl.ds(row_of(zl_, y_, c), ROWS_A)]

    def piece_b(zl_, y_):
        return weight.at[pl.ds(pl.multiple_of(row_of(zl_, y_, c) + ROWS_A, 16), SHARD - ROWS_A)]

    def send(ref, recv_sem, dev, cond):
        copy = pltpu.make_async_remote_copy(
            src_ref=ref, dst_ref=ref, send_sem=ag_send.at[len(sends)], recv_sem=recv_sem,
            device_id=dev, device_id_type=MESH,
        )
        sends.append((copy, cond))
        if cond is None:
            copy.start()
        else:
            pl.when(cond)(copy.start)

    def arrived(ref, recv_sem, cond):
        copy = pltpu.make_async_remote_copy(
            src_ref=ref, dst_ref=ref, send_sem=ag_send.at[0], recv_sem=recv_sem,
            device_id=partner, device_id_type=MESH,
        )
        if cond is None:
            copy.wait_recv()
        else:
            pl.when(cond)(copy.wait_recv)

    def both(a, b):
        return b if a is None else jnp.logical_and(a, b)

    def in_line(z_):
        return jnp.logical_and(z_ >= 0, z_ < NZ)

    def origins(distance):
        if distance == 0:
            return [(0, zl, None)]
        if not 0 < distance < NZ:
            return []
        return [(sign, lax.rem(zl + sign * distance + 2 * NZ, NZ), in_line(zl + sign * distance)) for sign in (-1, 1)]

    def even(v):
        return lax.rem(v, 2) == 0

    def odd(v):
        return lax.rem(v, 2) == 1

    def spread_b(y_):
        for sign in (1, -1):
            send(piece_b(zl, y_), zb_recv.at[zl * NY + y_], z_dev(sign), in_line(zl + sign))

    ring_sides = ((y_dn, y_up, even), (y_up, y_dn, odd))
    for sign in (1, -1):
        send(piece_a(zl, y), za_recv.at[zl], z_dev(sign), in_line(zl + sign))
    spread_b(y)
    for y_ in (y_up, y_dn):
        send(piece_b(zl, y), yb_recv.at[y], device(zl, y_, c), None)
    for y_ in (y_up, y_dn):
        send(piece_a(zl, y), ya_recv.at[zl * NY + y], device(zl, y_, c), None)
    send(own_rows, pair_recv, partner, None)

    def line_a(distance):
        for sign, o, there in origins(distance):
            arrived(piece_a(o, y), za_recv.at[o], there)
            send(piece_a(o, y), za_recv.at[o], z_dev(-sign), both(there, in_line(zl - sign)))
            for y_ in (y_up, y_dn):
                send(piece_a(o, y), ya_recv.at[o * NY + y], device(zl, y_, c), there)
            send(piece_a(o, y), pair_recv, partner, there)

    def ring_a(distance):
        for sign, o, there in origins(distance):
            for y_from, y_to, turn in ring_sides:
                arrived(piece_a(o, y_from), ya_recv.at[o * NY + y_from], there)
                send(piece_a(o, y_from), ya_recv.at[o * NY + y_from], device(zl, y_to, c), both(there, turn(o)))
                send(piece_a(o, y_from), pair_recv, partner, there)

    def far_a(distance):
        for sign, o, there in origins(distance):
            arrived(piece_a(o, y_far), ya_recv.at[o * NY + y_far], there)
            send(piece_a(o, y_far), pair_recv, partner, there)

    def ring_b():
        for y_from, y_to, turn in ring_sides:
            arrived(piece_b(zl, y_from), yb_recv.at[y_from], None)
            send(piece_b(zl, y_from), yb_recv.at[y_from], device(zl, y_to, c), turn(zl))
            spread_b(y_from)
            send(piece_b(zl, y_from), pair_recv, partner, None)

    def far_b():
        arrived(piece_b(zl, y_far), yb_recv.at[y_far], None)
        spread_b(y_far)
        send(piece_b(zl, y_far), pair_recv, partner, None)

    def line_b(distance):
        for sign, o, there in origins(distance):
            for y_ in (y, y_dn, y_up, y_far):
                arrived(piece_b(o, y_), zb_recv.at[o * NY + y_], there)
                send(piece_b(o, y_), zb_recv.at[o * NY + y_], z_dev(-sign), both(there, in_line(zl - sign)))
                send(piece_b(o, y_), pair_recv, partner, there)

    line_a(1)
    ring_b()
    line_a(2)
    ring_a(0)
    ring_a(1)
    far_b()
    line_a(3)
    line_b(1)
    ring_a(2)
    ring_a(3)
    line_b(2)
    far_a(1)
    far_a(0)
    far_a(2)
    far_a(3)
    line_b(3)
    arrived(weight.at[pl.ds(0, D // 2)], pair_recv, None)

    load_hist.wait()
    pl.when(is_first)(load_first.wait)
    pl.when(is_last)(load_up.wait)
    gain_acc[...] = jnp.zeros_like(gain_acc)

    def remote(src_ref, dst_ref, send_sem, recv_sem, dev):
        return pltpu.make_async_remote_copy(
            src_ref=src_ref, dst_ref=dst_ref, send_sem=send_sem, recv_sem=recv_sem,
            device_id=dev, device_id_type=MESH,
        )

    def rms(x):
        return lax.rsqrt(jnp.mean(x * x, axis=-1, keepdims=True) + 1e-05)

    def coded(v):
        scale = (jnp.max(jnp.abs(v), axis=-1, keepdims=True) + 1e-06).astype(bf16).astype(f32)
        return (v * (1.0 / scale)).astype(bf16).astype(f32) * scale, scale

    def rows_at(m):
        return pl.ds(pl.multiple_of(m * MR, MR), MR)

    every, low, high = pl.ds(0, D), pl.ds(0, HALF), pl.ds(HALF, HALF)

    def forward_rows(m, size, sending):
        rows = pl.ds(pl.multiple_of(m * MR, MR), size)

        @pl.when(has_prev)
        def _():
            for k in range(size // MR):
                part = rows_at(m + k)
                remote(x_out.at[part], x_in.at[part], f_send.at[m + k], f_recv.at[m + k], prev_dev).wait_recv()

        x = x_in[rows, :].astype(f32)
        inverse = rms(x)
        inv_buf[rows, :] = jnp.broadcast_to(inverse, (size, BLOCK))
        nrm = (x * inverse * gain[...]).astype(bf16)
        normed[rows, :] = nrm
        slot = ids[0, m * MR // SEQ]
        old_rows = pl.ds(pl.multiple_of(lax.rem(m * MR, SEQ), MR), size)
        lane = lax.broadcasted_iota(jnp.int32, (size, BLOCK), 1)
        scale_rows = jnp.zeros((size, BLOCK), f32)

        def mixed(n):
            return jnp.dot(nrm, weight[:, n * COLS : (n + 1) * COLS], preferred_element_type=f32)

        ahead = mixed(0)
        for n in range(D // COLS):
            cols = slice(n * COLS, (n + 1) * COLS)
            z = ahead
            if n + 1 < D // COLS:
                ahead = mixed(n + 1)
            sig = 0.5 + 0.5 * jnp.tanh(0.5 * z)
            factor[rows, cols] = sig * (1.0 + z * (1.0 - sig))
            res = (x_in[rows, cols].astype(f32) + z * sig).astype(bf16)
            out[rows, cols] = res
            old = hist[slot, old_rows, cols].astype(f32)
            delta = res.astype(f32) - old
            for b in range(COLS // BLOCK):
                part = slice(b * BLOCK, (b + 1) * BLOCK)
                decoded, scale = coded(delta[:, part])
                scale_rows = jnp.where(lane == n * (COLS // BLOCK) + b, scale, scale_rows)
                if sending:
                    x_out[rows, n * COLS + b * BLOCK : n * COLS + (b + 1) * BLOCK] = (old[:, part] + decoded).astype(bf16)
            if sending:
                here = pl.ds(n * COLS, COLS)
                there = pl.ds(0, HALF)
                direct = remote(x_out.at[rows, here], x_in.at[rows, here], f_send.at[m], f_recv.at[m], next_dev)
                hop = remote(x_out.at[rows, low], f_relay.at[rows], f_send.at[m], rf_recv.at[m], at_section(0))
                hop2 = remote(x_out.at[rows, high], f_relay.at[rows], f_send.at[m], rf_recv.at[m], at_section(LAST))
                pl.when(direct_next)(direct.start)
                pl.when(s == NEAR)(hop.start)
                pl.when(s == NEAR)(hop2.start)
        scale_buf[rows, :] = scale_rows.astype(bf16)

    def backward_rows(m, size):
        rows = pl.ds(pl.multiple_of(m * MR, MR), size)

        @pl.when(has_next)
        def _():
            for k in range(size // MR):
                part = rows_at(m + k)
                remote(g_out.at[part], g_in.at[part], b_send.at[m + k], b_recv.at[m + k], next_dev).wait_recv()

        g = g_in[rows, :].astype(f32)
        dz = (g * factor[rows, :]).astype(bf16)
        dmixed[rows, :] = dz
        for k in range(size // MR):
            dz_copy(m + k).start()
        inverse = inv_buf[rows, 0:1]
        shared = jnp.zeros((size, BLOCK), f32)
        for n in range(D // COLS):
            cols = slice(n * COLS, (n + 1) * COLS)
            dn = jnp.dot(dz, weight_t[:, cols], preferred_element_type=f32)
            unit = x_in[rows, cols].astype(f32) * inverse
            du = dn * gain[:, cols]
            du_buf[0:size, cols] = du
            prod = du * unit
            for b in range(COLS // BLOCK):
                shared = shared + prod[:, b * BLOCK : (b + 1) * BLOCK]
            prod = dn * unit
            total = prod[0:8]
            for k in range(1, size // 8):
                total = total + prod[8 * k : 8 * k + 8]
            gain_acc[:, cols] += total

        @pl.when(has_prev)
        def _():
            mean = jnp.sum(shared, axis=-1, keepdims=True) * (1.0 / D)
            for n in range(D // COLS):
                for b in range(COLS // BLOCK):
                    part = slice(n * COLS + b * BLOCK, n * COLS + (b + 1) * BLOCK)
                    unit = x_in[rows, part].astype(f32) * inverse
                    dx = g_in[rows, part].astype(f32) + inverse * (du_buf[0:size, part] - unit * mean)
                    decoded, _ = coded(dx)
                    g_out[rows, part] = decoded.astype(bf16)
                here = pl.ds(n * COLS, COLS)
                there = pl.ds(0, HALF)
                for k in range(size // MR):
                    sub = rows_at(m + k)
                    direct = remote(g_out.at[sub, here], g_in.at[sub, here], b_send.at[m + k], b_recv.at[m + k], prev_dev)
                    pl.when(direct_prev)(direct.start)
                    if size == MR:
                        hop = remote(g_out.at[sub, low], b_relay.at[sub], b_send.at[m + k], rb_recv.at[m + k], at_section(0))
                        hop2 = remote(g_out.at[sub, high], b_relay.at[sub], b_send.at[m + k], rb_recv.at[m + k], at_section(LAST))
                        pl.when(s == OVER)(hop.start)
                        pl.when(s == OVER)(hop2.start)

    def dz_copy(m):
        here = rows_at(m)
        there = pl.ds(pl.multiple_of(TOK + m * MR, MR), MR)
        return remote(dmixed.at[here], dmixed.at[there], dz_send.at[m], dz_recv.at[m], partner)

    def relay_forward(m, _):
        rows = rows_at(m)

        def passed(cols):
            return remote(f_relay.at[rows], x_in.at[rows, cols], rf_send.at[m], f_recv.at[m], at_section(OVER))

        remote(f_relay.at[rows], f_relay.at[rows], rf_send.at[m], rf_recv.at[m], at_section(NEAR)).wait_recv()
        pl.when(is_first)(passed(low).start)
        pl.when(is_last)(passed(high).start)
        return 0

    def relay_backward(m, _):
        rows = rows_at(m)

        def passed(cols):
            return remote(b_relay.at[rows], g_in.at[rows, cols], rb_send.at[m], b_recv.at[m], at_section(NEAR))

        remote(b_relay.at[rows], b_relay.at[rows], rb_send.at[m], rb_recv.at[m], at_section(OVER)).wait_recv()
        pl.when(is_first)(passed(low).start)
        pl.when(is_last)(passed(high).start)
        return 0

    def transpose_weight(i, _):
        rows = pl.ds(pl.multiple_of(i * 256, 256), 256)
        for j in range(D // 256):
            weight_t[j * 256 : (j + 1) * 256, rows] = weight[rows, j * 256 : (j + 1) * 256].T
        return 0

    def pack_normed(m, _):
        rows = rows_at(m)
        lane = lax.broadcasted_iota(jnp.int32, (MR, BLOCK), 1)
        for t in range(D // 256):
            a = normed[rows, 256 * t : 256 * t + 128].astype(f32)
            b = normed[rows, 256 * t + 128 : 256 * t + 256].astype(f32)
            zero = jnp.where(lane < SHARD, a, pltpu.roll(b, SHARD, 1))
            one = jnp.where(lane < SHARD, pltpu.roll(a, SHARD, 1), b)
            pack[rows, 128 * t : 128 * t + 128] = jnp.where(c == 0, zero, one).astype(bf16)
            pack_out[rows, 128 * t : 128 * t + 128] = jnp.where(c == 0, one, zero).astype(bf16)
        return 0

    pack_copy = remote(pack_out, pack.at[pl.ds(TOK, TOK)], pack_sems.at[0], pack_sems.at[1], partner)

    def forward_step(m, _):
        forward_rows(m, MR, True)
        return 0

    def backward_step(m, _):
        backward_rows(m, MR)
        return 0

    def turn_step(i, _):
        forward_rows(i * (WIDE // MR), WIDE, False)
        backward_rows(i * (WIDE // MR), WIDE)
        return 0

    @pl.when(s >= OVER)
    def _():
        lax.fori_loop(0, D // 256, transpose_weight, 0)

    @pl.when(is_last)
    def _():
        lax.fori_loop(0, MICRO, relay_forward, 0)
        lax.fori_loop(0, TOK // WIDE, turn_step, 0)
        lax.fori_loop(0, MICRO, relay_backward, 0)

    @pl.when(has_next)
    def _():
        lax.fori_loop(0, MICRO, forward_step, 0)

        @pl.when(is_first)
        def _():
            lax.fori_loop(0, MICRO, relay_forward, 0)

        @pl.when(s < OVER)
        def _():
            lax.fori_loop(0, D // 256, transpose_weight, 0)
            lax.fori_loop(0, MICRO, pack_normed, 0)
            pack_copy.start()

        @pl.when(is_first)
        def _():
            lax.fori_loop(0, MICRO, relay_backward, 0)

        lax.fori_loop(0, MICRO, backward_step, 0)

    @pl.when(s >= OVER)
    def _():
        lax.fori_loop(0, MICRO, pack_normed, 0)
        pack_copy.start()

    pack_copy.wait_recv()
    for m in range(MICRO):
        dz_copy(m).wait_recv()
    scatter = []

    def hand(src_ref, dst_ref, recv_sem, dev, cond=None):
        copy = remote(src_ref, dst_ref, rs_send.at[len(scatter)], recv_sem, dev)
        scatter.append((copy, cond))
        if cond is None:
            copy.start()
        else:
            pl.when(cond)(copy.start)

    def landed(ref, recv_sem, cond=None):
        copy = remote(ref, ref, rs_send.at[0], recv_sem, partner)
        if cond is None:
            copy.wait_recv()
        else:
            pl.when(cond)(copy.wait_recv)

    def add_to(ref, *terms):
        total = ref[...].astype(f32)
        for term in terms:
            total = total + term[...].astype(f32)
        ref[...] = total.astype(ref.dtype)

    low_half = zl < 2
    order = (
        jnp.where(low_half, 3, 0), jnp.where(low_half, 2, 1), jnp.where(low_half, 1 - zl, 5 - zl), zl,
    )
    up_dev, dn_dev = device(zl, y_up, c), device(zl, y_dn, c)

    def line(k):
        right = order[k] > zl
        upstream = jnp.where(right, zl > 0, zl < NZ - 1)
        return right, upstream, jnp.where(right, 0, 1)

    b_order = (y_far, y_up, y_dn, y)

    def b_rows(y_):
        return pl.ds(pl.multiple_of(y_ * ROWS_B, ROWS_B), ROWS_B)

    def send_line_b(k, yd, cond):
        right, _, side = line(k)
        zd = order[k]
        for step, way in ((1, right), (-1, jnp.logical_not(right))):
            hand(
                part_b.at[zd, b_rows(yd)], zb_in.at[side, zd, b_rows(yd)],
                lineb_recv.at[(side * NZ + zd) * NY + yd], z_dev(step), both(cond, way),
            )

    def send_line_a(k, cond):
        right, _, side = line(k)
        zd = order[k]
        for step, way in ((1, right), (-1, jnp.logical_not(right))):
            hand(part_a.at[zd, y], z_in.at[side, zd], line_recv.at[side * NZ + zd], z_dev(step), both(cond, way))

    def pass_line_b(k):
        _, upstream, side = line(k)
        zd = order[k]
        for yd in b_order:
            landed(zb_in.at[side, zd, b_rows(yd)], lineb_recv.at[(side * NZ + zd) * NY + yd], upstream)

            @pl.when(upstream)
            def _():
                add_to(part_b.at[zd, b_rows(yd)], zb_in.at[side, zd, b_rows(yd)])

            send_line_b(k, yd, upstream)

    def own_line_b():
        for yd in b_order:
            for side, there in ((0, zl > 0), (1, zl < NZ - 1)):
                landed(zb_in.at[side, zl, b_rows(yd)], lineb_recv.at[(side * NZ + zl) * NY + yd], there)

                @pl.when(there)
                def _():
                    add_to(part_b.at[zl, b_rows(yd)], zb_in.at[side, zl, b_rows(yd)])

            if yd is y_far:
                for dev, way in ((up_dev, even(zl)), (dn_dev, odd(zl))):
                    hand(part_b.at[zl, b_rows(y_far)], yb_far_in, farb_recv, dev, way)

    def own_line_a():
        for side, there in ((0, zl > 0), (1, zl < NZ - 1)):
            landed(z_in.at[side, zl], line_recv.at[side * NZ + zl], there)

            @pl.when(there)
            def _():
                weight_grad[0:ROWS_A, :] += z_in[side, zl].astype(f32)

    def ring_b_out():
        landed(yb_far_in, farb_recv)
        add_to(part_b.at[zl, b_rows(jnp.where(even(zl), y_up, y_dn))], yb_far_in)
        hand(part_b.at[zl, b_rows(y_up)], yb_in.at[0], ringb_recv.at[0], up_dev)
        hand(part_b.at[zl, b_rows(y_dn)], yb_in.at[1], ringb_recv.at[1], dn_dev)

    def ring_b_in():
        for side in range(2):
            landed(yb_in.at[side], ringb_recv.at[side])
        weight_grad[ROWS_A:SHARD, :] = (
            part_b[zl, b_rows(y)].astype(f32) + yb_in[0].astype(f32) + yb_in[1].astype(f32)
        )

    def pass_line_a(k):
        _, upstream, side = line(k)
        zd = order[k]
        landed(z_in.at[side, zd], line_recv.at[side * NZ + zd], upstream)

        @pl.when(upstream)
        def _():
            add_to(part_a.at[zd, y], z_in.at[side, zd])

        send_line_a(k, upstream)

    def ring_out(k):
        zd = order[k]
        landed(y_far_in.at[zd], far_recv.at[zd])
        target = jnp.where(even(zd), y_up, y_dn)
        add_to(part_a.at[zd, target], y_far_in.at[zd])
        hand(part_a.at[zd, y_up], y_in.at[zd, 0], ring_recv.at[zd * 2], up_dev)
        hand(part_a.at[zd, y_dn], y_in.at[zd, 1], ring_recv.at[zd * 2 + 1], dn_dev)

    def ring_in(k):
        zd = order[k]
        for side in range(2):
            landed(y_in.at[zd, side], ring_recv.at[zd * 2 + side])
        if k < NZ - 1:
            add_to(part_a.at[zd, y], y_in.at[zd, 0], y_in.at[zd, 1])
            send_line_a(k, jnp.logical_not(line(k)[1]))
        else:
            weight_grad[0:ROWS_A, :] = (
                part_a[zd, y].astype(f32) + y_in[zd, 0].astype(f32) + y_in[zd, 1].astype(f32)
            )

    gain_steps = (
        partner, device(zl, jnp.where(even(y), y + 1, y - 1), c), device(zl, y_far, c),
        device(jnp.where(even(zl), zl + 1, zl - 1), y, c), z_skip,
    )
    gain_buf[0] = jnp.sum(gain_acc[...], axis=0, keepdims=True)

    def gain_copy(k):
        return remote(gain_buf.at[k], gain_buf.at[6 + k], gain_send.at[k], gain_recv.at[k], gain_steps[k])

    def gain_add(k):
        gain_copy(k).wait_recv()
        gain_buf[k + 1] = gain_buf[k] + gain_buf[6 + k]
        if k + 1 < len(gain_steps):
            gain_copy(k + 1).start()

    def produce(k):
        zd = order[k]
        cols = pl.ds(pl.multiple_of(zd * 256, 256), 256)
        total = lax.dot_general(pack[:, cols], dmixed[...], (((0,), (0,)), ((), ())), preferred_element_type=f32).astype(bf16)
        for j in range(NY):
            part_a[zd, j] = total[j * SHARD : j * SHARD + ROWS_A]
            part_b[zd, j * ROWS_B : (j + 1) * ROWS_B] = total[j * SHARD + ROWS_A : (j + 1) * SHARD]
        for dev, way in ((up_dev, even(zd)), (dn_dev, odd(zd))):
            hand(part_a.at[zd, y_far], y_far_in.at[zd], far_recv.at[zd], dev, way)
        if k < NZ - 1:
            for yd in b_order:
                send_line_b(k, yd, jnp.logical_not(line(k)[1]))

    produce(0)
    gain_copy(0).start()
    produce(1)
    produce(3)
    ring_out(0)
    pass_line_b(0)
    gain_add(0)
    produce(2)
    ring_out(1)
    pass_line_b(2)
    ring_out(2)
    gain_add(1)
    ring_in(0)
    ring_out(3)
    pass_line_b(1)
    gain_add(2)
    pass_line_a(0)
    ring_in(1)
    own_line_b()
    gain_add(3)
    pass_line_a(1)
    ring_in(2)
    gain_add(4)
    pass_line_a(2)
    ring_in(3)
    ring_b_out()
    ring_b_in()
    own_line_a()

    gain_out[...] = gain_buf[5]
    scales[...] = scale_buf[:, : D // BLOCK]

    def drain(m, _):
        rows = rows_at(m)
        dz_copy(m).wait_send()

        @pl.when(has_next)
        def _():
            remote(x_out.at[rows], x_in.at[rows], f_send.at[m], f_recv.at[m], next_dev).wait_send()

        @pl.when(has_prev)
        def _():
            remote(g_out.at[rows], g_in.at[rows], b_send.at[m], b_recv.at[m], prev_dev).wait_send()

        @pl.when(ends)
        def _():
            remote(f_relay.at[rows], f_relay.at[rows], rf_send.at[m], rf_recv.at[m], at_section(OVER)).wait_send()
            remote(b_relay.at[rows], b_relay.at[rows], rb_send.at[m], rb_recv.at[m], at_section(NEAR)).wait_send()

        return 0

    lax.fori_loop(0, MICRO, drain, 0)
    pack_copy.wait_send()
    for k in range(len(gain_steps)):
        gain_copy(k).wait_send()
    for copy, cond in sends + scatter:
        if cond is None:
            copy.wait_send()
        else:
            pl.when(cond)(copy.wait_send)


def body(first_input, upstream, history, example_ids, norm_gain, weight):
    vmem = pl.BlockSpec(memory_space=pltpu.VMEM)
    anywhere = pl.BlockSpec(memory_space=pl.ANY)
    smem = pl.BlockSpec(memory_space=pltpu.SMEM)
    dma = pltpu.SemaphoreType.DMA
    out, scales, weight_grad, gain_grad = pl.pallas_call(
        relay_kernel,
        out_shape=(
            jax.ShapeDtypeStruct((TOK, D), bf16),
            jax.ShapeDtypeStruct((TOK, D // BLOCK), bf16),
            jax.ShapeDtypeStruct((SHARD, D), f32),
            jax.ShapeDtypeStruct((1, D), f32),
        ),
        in_specs=[anywhere, anywhere, anywhere, smem, vmem, anywhere],
        out_specs=(vmem,) * 4,
        scratch_shapes=[
            pltpu.VMEM((D, D), bf16),
            pltpu.VMEM((D, D), bf16),
            pltpu.VMEM((4, SEQ, D), bf16),
            pltpu.VMEM((TOK, D), bf16),
            pltpu.VMEM((TOK, D), bf16),
            pltpu.VMEM((TOK, D), bf16),
            pltpu.VMEM((TOK, D), bf16),
            pltpu.VMEM((TOK, HALF), bf16),
            pltpu.VMEM((TOK, HALF), bf16),
            pltpu.VMEM((TOK, D), f32),
            pltpu.VMEM((TOK, D), bf16),
            pltpu.VMEM((TOK, BLOCK), f32),
            pltpu.VMEM((WIDE, D), f32),
            pltpu.VMEM((TOK, BLOCK), bf16),
            pltpu.VMEM((8, D), f32),
            pltpu.VMEM((11, 1, D), f32),
            pltpu.VMEM((2 * TOK, HALF), bf16),
            pltpu.VMEM((TOK, HALF), bf16),
            pltpu.VMEM((2 * TOK, D), bf16),
            pltpu.VMEM((NZ, NY, ROWS_A, D), bf16),
            pltpu.VMEM((NZ, NY * ROWS_B, D), bf16),
            pltpu.VMEM((NZ, ROWS_A, D), bf16),
            pltpu.VMEM((NZ, 2, ROWS_A, D), bf16),
            pltpu.VMEM((2, NZ, ROWS_A, D), bf16),
            pltpu.VMEM((2, NZ, NY * ROWS_B, D), bf16),
            pltpu.VMEM((ROWS_B, D), bf16),
            pltpu.VMEM((2, ROWS_B, D), bf16),
            dma((4,)),
            dma((MICRO,)), dma((MICRO,)), dma((MICRO,)), dma((MICRO,)),
            dma((MICRO,)), dma((MICRO,)), dma((MICRO,)), dma((MICRO,)),
            dma((NZ,)), dma((NZ * NY,)), dma((NY,)), dma((NZ * NY,)), dma(()), dma((136,)),
            dma((2,)), dma((MICRO,)), dma((MICRO,)), dma((5,)), dma((5,)),
            dma((96,)), dma((NZ,)), dma((NZ * 2,)), dma((2 * NZ,)), dma((2 * NZ * NY,)), dma(()), dma((2,)),
        ],
        compiler_params=pltpu.CompilerParams(
            collective_id=0, has_side_effects=True, vmem_limit_bytes=56 * 2**20
        ),
    )(first_input, upstream, history, example_ids, norm_gain, weight)
    return (out[None], scales[None], weight_grad[None], gain_grad)


def solution(mesh):
    return jax.shard_map(
        body,
        mesh=mesh,
        in_specs=(
            P("dp", None),
            P("dp", None),
            P("section", None, "dp", None, None),
            P("dp", None),
            P("section", None),
            P("section", "dp", None),
        ),
        out_specs=(
            P("section", "dp", None),
            P("section", "dp", None),
            P("section", "dp", None),
            P("section", None),
        ),
        check_vma=False,
    )
```

```python
import functools

import jax
import jax.numpy as jnp
from jax import lax
from jax.experimental import pallas as pl
from jax.experimental.pallas import tpu as pltpu
from jax.sharding import PartitionSpec as P

MESH = pl.DeviceIdType.MESH
D = 2048
TOK = 256
SEQ = 64
BLOCK = 128
N_SECTION = 8
NZ = 4
NY = 4
SHARD = 64
ROWS_A = 48
ROWS_B = SHARD - ROWS_A
MICRO = 16
MR = TOK // MICRO
WIDE = 32
HALF = D // 2
LAST = N_SECTION - 1
NEAR, OVER = 3, 4
LEAD_0 = 14
LEAD_7 = 16
BACK_0 = 16
BACK_7 = 0
COLS = 512
SENT = 1024
bf16 = jnp.bfloat16
f32 = jnp.float32


def relay_kernel(
    first_hbm, up_hbm, hist_hbm, ids, gain, w_hbm,
    out, scales, weight_grad, gain_out,
    shards, weight_t, hist, x_in, g_in, x_out, g_out, f_relay, b_relay, factor, normed, inv_buf, du_buf, scale_buf, gain_acc, gain_buf,
    pack, pack_out, dmixed, part_a, part_b, y_far_in, y_in, z_in, zb_in, yb_far_in, yb_in,
    local_sem, f_send, f_recv, b_send, b_recv, rf_send, rf_recv, rb_send, rb_recv,
    za_recv, ya_recv, yb_recv, zb_recv, pair_recv, ag_send,
    pack_sems, dz_send, dz_recv, gain_send, gain_recv,
    rs_send, far_recv, ring_recv, line_recv, lineb_recv, farb_recv, ringb_recv,
):
    dp = lax.axis_index("dp")
    s = lax.axis_index("section")
    zl = dp // 8
    y = lax.rem(dp // 2, NY)
    c = lax.rem(dp, 2)

    def device(zl_, y_, c_):
        return (zl_ * 8 + y_ * 2 + c_, s)

    def at_section(s_):
        return (dp, s_)

    y_up, y_dn, y_far = lax.rem(y + 1, NY), lax.rem(y + 3, NY), lax.rem(y + 2, NY)
    partner = device(zl, y, 1 - c)
    prev_dev, next_dev = at_section(lax.rem(s + 7, 8)), at_section(lax.rem(s + 1, 8))
    is_first, is_last = s == 0, s == LAST
    has_prev, has_next = s > 0, s < LAST
    direct_prev = jnp.logical_and(has_prev, s != OVER)
    direct_next = jnp.logical_and(has_next, s != NEAR)

    def z_dev(step):
        return device(lax.rem(zl + step + NZ, NZ), y, c)

    weight = shards.reshape(D, D)

    own_rows = shards.at[zl, y, c]
    load_w = pltpu.make_async_copy(w_hbm.at[0], own_rows, local_sem.at[0])
    load_w.start()
    load_hist = pltpu.make_async_copy(hist_hbm.at[0, 0], hist, local_sem.at[1])
    load_hist.start()
    load_first = pltpu.make_async_copy(first_hbm, x_in, local_sem.at[2])
    load_up = pltpu.make_async_copy(up_hbm, g_in, local_sem.at[3])
    pl.when(is_first)(load_first.start)
    pl.when(is_last)(load_up.start)

    barrier = pltpu.get_barrier_semaphore()
    z_skip = device(lax.rem(zl + 2, NZ), y, c)
    for dev in (partner, device(zl, y_up, c), device(zl, y_dn, c), device(zl, y_far, c), z_skip):
        pl.semaphore_signal(barrier, inc=1, device_id=dev, device_id_type=MESH)
    ends = jnp.logical_or(is_first, is_last)
    middle = jnp.logical_or(s == NEAR, s == OVER)
    others = (
        (z_dev(-1), zl > 0), (z_dev(1), zl < NZ - 1), (prev_dev, direct_prev), (next_dev, direct_next),
        (at_section(NEAR), ends), (at_section(OVER), ends), (at_section(0), middle), (at_section(LAST), middle),
    )
    greeted = jnp.int32(5)
    for dev, there in others:
        greeted = greeted + there.astype(jnp.int32)

        @pl.when(there)
        def _():
            pl.semaphore_signal(barrier, inc=1, device_id=dev, device_id_type=MESH)

    pl.semaphore_wait(barrier, greeted)
    load_w.wait()

    sends = []

    def piece_a(zl_, y_):
        return shards.at[zl_, y_, c, pl.ds(0, ROWS_A)]

    def piece_b(zl_, y_):
        return shards.at[zl_, y_, c, pl.ds(ROWS_A, ROWS_B)]

    def send(ref, recv_sem, dev, cond):
        copy = pltpu.make_async_remote_copy(
            src_ref=ref, dst_ref=ref, send_sem=ag_send.at[len(sends)], recv_sem=recv_sem,
            device_id=dev, device_id_type=MESH,
        )
        sends.append((copy, cond))
        if cond is None:
            copy.start()
        else:
            pl.when(cond)(copy.start)

    def arrived(ref, recv_sem, cond):
        copy = pltpu.make_async_remote_copy(
            src_ref=ref, dst_ref=ref, send_sem=ag_send.at[0], recv_sem=recv_sem,
            device_id=partner, device_id_type=MESH,
        )
        if cond is None:
            copy.wait_recv()
        else:
            pl.when(cond)(copy.wait_recv)

    def both(a, b):
        return b if a is None else jnp.logical_and(a, b)

    def in_line(z_):
        return jnp.logical_and(z_ >= 0, z_ < NZ)

    def origins(distance):
        if distance == 0:
            return [(0, zl, None)]
        if not 0 < distance < NZ:
            return []
        return [(sign, lax.rem(zl + sign * distance + 2 * NZ, NZ), in_line(zl + sign * distance)) for sign in (-1, 1)]

    def even(v):
        return lax.rem(v, 2) == 0

    def odd(v):
        return lax.rem(v, 2) == 1

    def spread_b(y_):
        for sign in (1, -1):
            send(piece_b(zl, y_), zb_recv.at[zl * NY + y_], z_dev(sign), in_line(zl + sign))

    ring_sides = ((y_dn, y_up, even), (y_up, y_dn, odd))
    for sign in (1, -1):
        send(piece_a(zl, y), za_recv.at[zl], z_dev(sign), in_line(zl + sign))
    spread_b(y)
    for y_ in (y_up, y_dn):
        send(piece_b(zl, y), yb_recv.at[y], device(zl, y_, c), None)
    for y_ in (y_up, y_dn):
        send(piece_a(zl, y), ya_recv.at[zl * NY + y], device(zl, y_, c), None)
    send(own_rows, pair_recv, partner, None)

    def line_a(distance):
        for sign, o, there in origins(distance):
            arrived(piece_a(o, y), za_recv.at[o], there)
            send(piece_a(o, y), za_recv.at[o], z_dev(-sign), both(there, in_line(zl - sign)))
            for y_ in (y_up, y_dn):
                send(piece_a(o, y), ya_recv.at[o * NY + y], device(zl, y_, c), there)
            send(piece_a(o, y), pair_recv, partner, there)

    def ring_a(distance):
        for sign, o, there in origins(distance):
            for y_from, y_to, turn in ring_sides:
                arrived(piece_a(o, y_from), ya_recv.at[o * NY + y_from], there)
                send(piece_a(o, y_from), ya_recv.at[o * NY + y_from], device(zl, y_to, c), both(there, turn(o)))
                send(piece_a(o, y_from), pair_recv, partner, there)

    def far_a(distance):
        for sign, o, there in origins(distance):
            arrived(piece_a(o, y_far), ya_recv.at[o * NY + y_far], there)
            send(piece_a(o, y_far), pair_recv, partner, there)

    def ring_b():
        for y_from, y_to, turn in ring_sides:
            arrived(piece_b(zl, y_from), yb_recv.at[y_from], None)
            send(piece_b(zl, y_from), yb_recv.at[y_from], device(zl, y_to, c), turn(zl))
            spread_b(y_from)
            send(piece_b(zl, y_from), pair_recv, partner, None)

    def far_b():
        arrived(piece_b(zl, y_far), yb_recv.at[y_far], None)
        spread_b(y_far)
        send(piece_b(zl, y_far), pair_recv, partner, None)

    def line_b(distance):
        for sign, o, there in origins(distance):
            for y_ in (y, y_dn, y_up, y_far):
                arrived(piece_b(o, y_), zb_recv.at[o * NY + y_], there)
                send(piece_b(o, y_), zb_recv.at[o * NY + y_], z_dev(-sign), both(there, in_line(zl - sign)))
                send(piece_b(o, y_), pair_recv, partner, there)

    line_a(1)
    ring_b()
    line_a(2)
    far_b()
    ring_a(0)
    ring_a(1)
    line_a(3)
    line_b(1)
    ring_a(2)
    ring_a(3)
    line_b(2)
    far_a(2)
    line_b(3)
    far_a(1)
    far_a(0)
    far_a(3)
    arrived(shards.at[pl.ds(0, NZ), pl.ds(0, NY), 1 - c], pair_recv, None)

    load_hist.wait()
    pl.when(is_first)(load_first.wait)
    pl.when(is_last)(load_up.wait)
    gain_acc[...] = jnp.zeros_like(gain_acc)

    def remote(src_ref, dst_ref, send_sem, recv_sem, dev):
        return pltpu.make_async_remote_copy(
            src_ref=src_ref, dst_ref=dst_ref, send_sem=send_sem, recv_sem=recv_sem,
            device_id=dev, device_id_type=MESH,
        )

    def rms(x):
        return lax.rsqrt(jnp.mean(x * x, axis=-1, keepdims=True) + 1e-05)

    def coded(v):
        scale = (jnp.max(jnp.abs(v), axis=-1, keepdims=True) + 1e-06).astype(bf16).astype(f32)
        return (v * (1.0 / scale)).astype(bf16).astype(f32) * scale, scale

    def rows_at(m):
        return pl.ds(pl.multiple_of(m * MR, MR), MR)

    every, low, high = pl.ds(0, D), pl.ds(0, HALF), pl.ds(HALF, HALF)

    def forward_rows(m, size, route):
        rows = pl.ds(pl.multiple_of(m * MR, MR), size)

        @pl.when(has_prev)
        def _():
            for k in range(size // MR):
                part = rows_at(m + k)
                remote(x_out.at[part], x_in.at[part], f_send.at[m + k], f_recv.at[m + k], prev_dev).wait_recv()

        x = x_in[rows, :].astype(f32)
        inverse = rms(x)
        inv_buf[rows, :] = jnp.broadcast_to(inverse, (size, BLOCK))
        nrm = (x * inverse * gain[...]).astype(bf16)
        normed[rows, :] = nrm
        slot = ids[0, m * MR // SEQ]
        old_rows = pl.ds(pl.multiple_of(lax.rem(m * MR, SEQ), MR), size)
        lane = lax.broadcasted_iota(jnp.int32, (size, BLOCK), 1)
        scale_rows = jnp.zeros((size, BLOCK), f32)

        def mixed(n):
            return jnp.dot(nrm, weight[:, n * COLS : (n + 1) * COLS], preferred_element_type=f32)

        ahead = mixed(0)
        for n in range(D // COLS):
            cols = slice(n * COLS, (n + 1) * COLS)
            z = ahead
            if n + 1 < D // COLS:
                ahead = mixed(n + 1)
            sig = 0.5 + 0.5 * jnp.tanh(0.5 * z)
            factor[rows, cols] = sig * (1.0 + z * (1.0 - sig))
            res = (x_in[rows, cols].astype(f32) + z * sig).astype(bf16)
            out[rows, cols] = res
            old = hist[slot, old_rows, cols].astype(f32)
            delta = res.astype(f32) - old
            for b in range(COLS // BLOCK):
                part = slice(b * BLOCK, (b + 1) * BLOCK)
                decoded, scale = coded(delta[:, part])
                scale_rows = jnp.where(lane == n * (COLS // BLOCK) + b, scale, scale_rows)
                if route is not None:
                    x_out[rows, n * COLS + b * BLOCK : n * COLS + (b + 1) * BLOCK] = (old[:, part] + decoded).astype(bf16)
            if route is not None and (n + 1) * COLS % SENT == 0:
                start = (n + 1) * COLS - SENT
                here = pl.ds(start, SENT)
                if route == "direct":
                    remote(x_out.at[rows, here], x_in.at[rows, here], f_send.at[m], f_recv.at[m], next_dev).start()
                else:
                    via = at_section(0 if start < HALF else LAST)
                    there = pl.ds(start % HALF, SENT)
                    remote(x_out.at[rows, here], f_relay.at[rows, there], f_send.at[m], rf_recv.at[m], via).start()
        scale_buf[rows, :] = scale_rows

    def backward_rows(m, size, route):
        rows = pl.ds(pl.multiple_of(m * MR, MR), size)

        @pl.when(has_next)
        def _():
            for k in range(size // MR):
                part = rows_at(m + k)
                remote(g_out.at[part], g_in.at[part], b_send.at[m + k], b_recv.at[m + k], next_dev).wait_recv()

        g = g_in[rows, :].astype(f32)
        dz = (g * factor[rows, :]).astype(bf16)
        dmixed[rows, :] = dz
        for k in range(size // MR):
            dz_copy(m + k).start()
        inverse = inv_buf[rows, 0:1]
        shared = jnp.zeros((size, BLOCK), f32)
        for n in range(D // COLS):
            cols = slice(n * COLS, (n + 1) * COLS)
            dn = jnp.dot(dz, weight_t[:, cols], preferred_element_type=f32)
            unit = x_in[rows, cols].astype(f32) * inverse
            du = dn * gain[:, cols]
            du_buf[0:size, cols] = du
            prod = du * unit
            for b in range(COLS // BLOCK):
                shared = shared + prod[:, b * BLOCK : (b + 1) * BLOCK]
            prod = dn * unit
            total = prod[0:8]
            for k in range(1, size // 8):
                total = total + prod[8 * k : 8 * k + 8]
            gain_acc[:, cols] += total

        if route is None:
            return
        mean = jnp.sum(shared, axis=-1, keepdims=True) * (1.0 / D)
        for n in range(D // SENT):
            for b in range(SENT // BLOCK):
                part = slice(n * SENT + b * BLOCK, n * SENT + (b + 1) * BLOCK)
                unit = x_in[rows, part].astype(f32) * inverse
                dx = g_in[rows, part].astype(f32) + inverse * (du_buf[0:size, part] - unit * mean)
                decoded, _ = coded(dx)
                g_out[rows, part] = decoded.astype(bf16)
            here = pl.ds(n * SENT, SENT)
            for k in range(size // MR):
                sub = rows_at(m + k)
                if route == "direct":
                    remote(g_out.at[sub, here], g_in.at[sub, here], b_send.at[m + k], b_recv.at[m + k], prev_dev).start()
                else:
                    via = at_section(0 if n * SENT < HALF else LAST)
                    there = pl.ds(n * SENT % HALF, SENT)
                    remote(g_out.at[sub, here], b_relay.at[sub, there], b_send.at[m + k], rb_recv.at[m + k], via).start()

    def dz_copy(m):
        here = rows_at(m)
        there = pl.ds(pl.multiple_of(TOK + m * MR, MR), MR)
        return remote(dmixed.at[here], dmixed.at[there], dz_send.at[m], dz_recv.at[m], partner)

    def relay_forward(m, _):
        rows = rows_at(m)

        def passed(cols):
            return remote(f_relay.at[rows], x_in.at[rows, cols], rf_send.at[m], f_recv.at[m], at_section(OVER))

        remote(f_relay.at[rows], f_relay.at[rows], rf_send.at[m], rf_recv.at[m], at_section(NEAR)).wait_recv()
        pl.when(is_first)(passed(low).start)
        pl.when(is_last)(passed(high).start)
        return 0

    def relay_backward(m, _):
        rows = rows_at(m)

        def passed(cols):
            return remote(b_relay.at[rows], g_in.at[rows, cols], rb_send.at[m], b_recv.at[m], at_section(NEAR))

        remote(b_relay.at[rows], b_relay.at[rows], rb_send.at[m], rb_recv.at[m], at_section(OVER)).wait_recv()
        pl.when(is_first)(passed(low).start)
        pl.when(is_last)(passed(high).start)
        return 0

    def transpose_weight(i, _):
        rows = pl.ds(pl.multiple_of(i * 256, 256), 256)
        for j in range(D // 256):
            weight_t[j * 256 : (j + 1) * 256, rows] = weight[rows, j * 256 : (j + 1) * 256].T
        return 0

    def pack_normed(m, _):
        rows = rows_at(m)
        lane = lax.broadcasted_iota(jnp.int32, (MR, BLOCK), 1)
        for t in range(D // 256):
            a = normed[rows, 256 * t : 256 * t + 128].astype(f32)
            b = normed[rows, 256 * t + 128 : 256 * t + 256].astype(f32)
            zero = jnp.where(lane < SHARD, a, pltpu.roll(b, SHARD, 1))
            one = jnp.where(lane < SHARD, pltpu.roll(a, SHARD, 1), b)
            pack[rows, 128 * t : 128 * t + 128] = jnp.where(c == 0, zero, one).astype(bf16)
            pack_out[rows, 128 * t : 128 * t + 128] = jnp.where(c == 0, one, zero).astype(bf16)
        return 0

    pack_copy = remote(pack_out, pack.at[pl.ds(TOK, TOK)], pack_sems.at[0], pack_sems.at[1], partner)

    def forward_all(route):
        def step(m, _):
            forward_rows(m, MR, route)
            if route == "direct":
                @pl.when(jnp.logical_and(is_first, m >= LEAD_0))
                def _():
                    relay_forward(m - LEAD_0, 0)
            return 0

        lax.fori_loop(0, MICRO, step, 0)

    def backward_all(route):
        def step(m, _):
            backward_rows(m, MR, route)
            if route is None:
                @pl.when(m < MICRO - BACK_0)
                def _():
                    relay_backward(m + BACK_0, 0)
            return 0

        lax.fori_loop(0, MICRO, step, 0)

    def turn_step(i, _):
        forward_rows(i * (WIDE // MR), WIDE, None)

        @pl.when(i < (MICRO - LEAD_7) // 2)
        def _():
            relay_forward(LEAD_7 + 2 * i, 0)

        backward_rows(i * (WIDE // MR), WIDE, "direct")

        @pl.when(i < (MICRO - LEAD_7) // 2)
        def _():
            relay_forward(LEAD_7 + 2 * i + 1, 0)

        @pl.when(i == TOK // WIDE - 2)
        def _():
            lax.fori_loop(0, BACK_7, relay_backward, 0)

        return 0

    @pl.when(s >= OVER)
    def _():
        lax.fori_loop(0, D // 256, transpose_weight, 0)

    @pl.when(is_last)
    def _():
        lax.fori_loop(0, LEAD_7, relay_forward, 0)
        lax.fori_loop(0, TOK // WIDE, turn_step, 0)
        lax.fori_loop(BACK_7, MICRO, relay_backward, 0)

    @pl.when(direct_next)
    def _():
        forward_all("direct")

    @pl.when(s == NEAR)
    def _():
        forward_all("relay")

    @pl.when(is_first)
    def _():
        lax.fori_loop(MICRO - LEAD_0, MICRO, relay_forward, 0)

    @pl.when(s < OVER)
    def _():
        lax.fori_loop(0, D // 256, transpose_weight, 0)
        lax.fori_loop(0, MICRO, pack_normed, 0)
        pack_copy.start()
        scales[...] = scale_buf[...].T[: D // BLOCK].astype(bf16)

    @pl.when(is_first)
    def _():
        lax.fori_loop(0, BACK_0, relay_backward, 0)
        backward_all(None)

    @pl.when(jnp.logical_and(direct_prev, has_next))
    def _():
        backward_all("direct")

    @pl.when(s == OVER)
    def _():
        backward_all("relay")

    @pl.when(s >= OVER)
    def _():
        lax.fori_loop(0, MICRO, pack_normed, 0)
        pack_copy.start()
        scales[...] = scale_buf[...].T[: D // BLOCK].astype(bf16)

    pack_copy.wait_recv()
    for m in range(MICRO):
        dz_copy(m).wait_recv()
    scatter = []

    def hand(src_ref, dst_ref, recv_sem, dev, cond=None):
        copy = remote(src_ref, dst_ref, rs_send.at[len(scatter)], recv_sem, dev)
        scatter.append((copy, cond))
        if cond is None:
            copy.start()
        else:
            pl.when(cond)(copy.start)

    def landed(ref, recv_sem, cond=None):
        copy = remote(ref, ref, rs_send.at[0], recv_sem, partner)
        if cond is None:
            copy.wait_recv()
        else:
            pl.when(cond)(copy.wait_recv)

    def add_to(ref, *terms):
        total = ref[...].astype(f32)
        for term in terms:
            total = total + term[...].astype(f32)
        ref[...] = total.astype(ref.dtype)

    low_half = zl < 2
    order = (
        jnp.where(low_half, 3, 0), jnp.where(low_half, 2, 1), jnp.where(low_half, 1 - zl, 5 - zl), zl,
    )
    up_dev, dn_dev = device(zl, y_up, c), device(zl, y_dn, c)

    def line(k):
        right = order[k] > zl
        upstream = jnp.where(right, zl > 0, zl < NZ - 1)
        return right, upstream, jnp.where(right, 0, 1)

    def b_rows(y_):
        return pl.ds(pl.multiple_of(y_ * ROWS_B, ROWS_B), ROWS_B)

    def send_line_b(k, cond):
        right, _, side = line(k)
        zd = order[k]
        for step, way in ((1, right), (-1, jnp.logical_not(right))):
            hand(part_b.at[zd], zb_in.at[side, zd], lineb_recv.at[side * NZ + zd], z_dev(step), both(cond, way))

    def send_line_a(k, cond):
        right, _, side = line(k)
        zd = order[k]
        for step, way in ((1, right), (-1, jnp.logical_not(right))):
            hand(part_a.at[zd, y], z_in.at[side, zd], line_recv.at[side * NZ + zd], z_dev(step), both(cond, way))

    def pass_line_b(k):
        _, upstream, side = line(k)
        zd = order[k]
        landed(zb_in.at[side, zd], lineb_recv.at[side * NZ + zd], upstream)

        @pl.when(upstream)
        def _():
            add_to(part_b.at[zd], zb_in.at[side, zd])

        send_line_b(k, upstream)

    def own_line_b():
        for side, there in ((0, zl > 0), (1, zl < NZ - 1)):
            landed(zb_in.at[side, zl], lineb_recv.at[side * NZ + zl], there)

            @pl.when(there)
            def _():
                add_to(part_b.at[zl], zb_in.at[side, zl])

        for dev, way in ((up_dev, even(zl)), (dn_dev, odd(zl))):
            hand(part_b.at[zl, b_rows(y_far)], yb_far_in, farb_recv, dev, way)

    def own_line_a():
        for side, there in ((0, zl > 0), (1, zl < NZ - 1)):
            landed(z_in.at[side, zl], line_recv.at[side * NZ + zl], there)

            @pl.when(there)
            def _():
                weight_grad[0:ROWS_A, :] += z_in[side, zl].astype(f32)

    def ring_b_out():
        landed(yb_far_in, farb_recv)
        add_to(part_b.at[zl, b_rows(jnp.where(even(zl), y_up, y_dn))], yb_far_in)
        hand(part_b.at[zl, b_rows(y_up)], yb_in.at[0], ringb_recv.at[0], up_dev)
        hand(part_b.at[zl, b_rows(y_dn)], yb_in.at[1], ringb_recv.at[1], dn_dev)

    def ring_b_in():
        for side in range(2):
            landed(yb_in.at[side], ringb_recv.at[side])
        weight_grad[ROWS_A:SHARD, :] = (
            part_b[zl, b_rows(y)].astype(f32) + yb_in[0].astype(f32) + yb_in[1].astype(f32)
        )

    def pass_line_a(k):
        _, upstream, side = line(k)
        zd = order[k]
        landed(z_in.at[side, zd], line_recv.at[side * NZ + zd], upstream)

        @pl.when(upstream)
        def _():
            add_to(part_a.at[zd, y], z_in.at[side, zd])

        send_line_a(k, upstream)

    def ring_out(k):
        zd = order[k]
        landed(y_far_in.at[zd], far_recv.at[zd])
        target = jnp.where(even(zd), y_up, y_dn)
        add_to(part_a.at[zd, target], y_far_in.at[zd])
        hand(part_a.at[zd, y_up], y_in.at[zd, 0], ring_recv.at[zd * 2], up_dev)
        hand(part_a.at[zd, y_dn], y_in.at[zd, 1], ring_recv.at[zd * 2 + 1], dn_dev)

    def ring_in(k):
        zd = order[k]
        for side in range(2):
            landed(y_in.at[zd, side], ring_recv.at[zd * 2 + side])
        if k < NZ - 1:
            add_to(part_a.at[zd, y], y_in.at[zd, 0], y_in.at[zd, 1])
            send_line_a(k, jnp.logical_not(line(k)[1]))
        else:
            weight_grad[0:ROWS_A, :] = (
                part_a[zd, y].astype(f32) + y_in[zd, 0].astype(f32) + y_in[zd, 1].astype(f32)
            )

    gain_steps = (
        partner, device(zl, jnp.where(even(y), y + 1, y - 1), c), device(zl, y_far, c),
        device(jnp.where(even(zl), zl + 1, zl - 1), y, c), z_skip,
    )
    gain_buf[0] = jnp.sum(gain_acc[...], axis=0, keepdims=True)

    def gain_copy(k):
        return remote(gain_buf.at[k], gain_buf.at[6 + k], gain_send.at[k], gain_recv.at[k], gain_steps[k])

    def gain_add(k):
        gain_copy(k).wait_recv()
        gain_buf[k + 1] = gain_buf[k] + gain_buf[6 + k]
        if k + 1 < len(gain_steps):
            gain_copy(k + 1).start()

    def produce(k):
        zd = order[k]
        cols = pl.ds(pl.multiple_of(zd * 256, 256), 256)
        total = lax.dot_general(pack[:, cols], dmixed[...], (((0,), (0,)), ((), ())), preferred_element_type=f32).astype(bf16)
        for j in range(NY):
            part_a[zd, j] = total[j * SHARD : j * SHARD + ROWS_A]
            part_b[zd, j * ROWS_B : (j + 1) * ROWS_B] = total[j * SHARD + ROWS_A : (j + 1) * SHARD]
        for dev, way in ((up_dev, even(zd)), (dn_dev, odd(zd))):
            hand(part_a.at[zd, y_far], y_far_in.at[zd], far_recv.at[zd], dev, way)
        if k < NZ - 1:
            send_line_b(k, jnp.logical_not(line(k)[1]))

    produce(0)
    gain_copy(0).start()
    produce(1)
    ring_out(0)
    produce(2)
    pass_line_b(0)
    gain_add(0)
    produce(3)
    ring_out(1)
    pass_line_b(1)
    ring_in(0)
    gain_add(1)
    ring_out(2)
    pass_line_b(2)
    ring_in(1)
    gain_add(2)
    pass_line_a(0)
    own_line_b()
    gain_add(3)
    ring_out(3)
    ring_in(2)
    gain_add(4)
    ring_b_out()
    pass_line_a(1)
    pass_line_a(2)
    ring_in(3)
    ring_b_in()
    own_line_a()

    gain_out[...] = gain_buf[5]

    def drain(m, _):
        rows = rows_at(m)
        dz_copy(m).wait_send()

        @pl.when(has_next)
        def _():
            remote(x_out.at[rows], x_in.at[rows], f_send.at[m], f_recv.at[m], next_dev).wait_send()

        @pl.when(has_prev)
        def _():
            remote(g_out.at[rows], g_in.at[rows], b_send.at[m], b_recv.at[m], prev_dev).wait_send()

        @pl.when(ends)
        def _():
            remote(f_relay.at[rows], f_relay.at[rows], rf_send.at[m], rf_recv.at[m], at_section(OVER)).wait_send()
            remote(b_relay.at[rows], b_relay.at[rows], rb_send.at[m], rb_recv.at[m], at_section(NEAR)).wait_send()

        return 0

    lax.fori_loop(0, MICRO, drain, 0)
    pack_copy.wait_send()
    for k in range(len(gain_steps)):
        gain_copy(k).wait_send()
    for copy, cond in sends + scatter:
        if cond is None:
            copy.wait_send()
        else:
            pl.when(cond)(copy.wait_send)


def hand_over(*refs):
    n = len(refs) // 2
    copies = []
    for src, dst in zip(refs[:n], refs[n : 2 * n]):
        rows = src.shape[0]
        pieces = 8 if rows * src.shape[1] >= 2**17 else 1
        for k in range(pieces):
            part = pl.ds(k * (rows // pieces), rows // pieces)
            copies.append(pltpu.make_async_copy(src.at[part], dst.at[part], refs[-1].at[len(copies)]))
    for copy in copies:
        copy.start()
    for copy in copies:
        copy.wait()


def body(first_input, upstream, history, example_ids, norm_gain, weight):
    vmem = pl.BlockSpec(memory_space=pltpu.VMEM)
    anywhere = pl.BlockSpec(memory_space=pl.ANY)
    smem = pl.BlockSpec(memory_space=pltpu.SMEM)
    dma = pltpu.SemaphoreType.DMA
    out, scales, weight_grad, gain_grad = pl.pallas_call(
        relay_kernel,
        out_shape=(
            jax.ShapeDtypeStruct((TOK, D), bf16),
            jax.ShapeDtypeStruct((D // BLOCK, TOK), bf16),
            jax.ShapeDtypeStruct((SHARD, D), f32),
            jax.ShapeDtypeStruct((1, D), f32),
        ),
        in_specs=[anywhere, anywhere, anywhere, smem, vmem, anywhere],
        out_specs=(vmem,) * 4,
        scratch_shapes=[
            pltpu.VMEM((NZ, NY, 2, SHARD, D), bf16),
            pltpu.VMEM((D, D), bf16),
            pltpu.VMEM((4, SEQ, D), bf16),
            pltpu.VMEM((TOK, D), bf16),
            pltpu.VMEM((TOK, D), bf16),
            pltpu.VMEM((TOK, D), bf16),
            pltpu.VMEM((TOK, D), bf16),
            pltpu.VMEM((TOK, HALF), bf16),
            pltpu.VMEM((TOK, HALF), bf16),
            pltpu.VMEM((TOK, D), f32),
            pltpu.VMEM((TOK, D), bf16),
            pltpu.VMEM((TOK, BLOCK), f32),
            pltpu.VMEM((WIDE, D), f32),
            pltpu.VMEM((TOK, BLOCK), f32),
            pltpu.VMEM((8, D), f32),
            pltpu.VMEM((11, 1, D), f32),
            pltpu.VMEM((2 * TOK, HALF), bf16),
            pltpu.VMEM((TOK, HALF), bf16),
            pltpu.VMEM((2 * TOK, D), bf16),
            pltpu.VMEM((NZ, NY, ROWS_A, D), bf16),
            pltpu.VMEM((NZ, NY * ROWS_B, D), bf16),
            pltpu.VMEM((NZ, ROWS_A, D), bf16),
            pltpu.VMEM((NZ, 2, ROWS_A, D), bf16),
            pltpu.VMEM((2, NZ, ROWS_A, D), bf16),
            pltpu.VMEM((2, NZ, NY * ROWS_B, D), bf16),
            pltpu.VMEM((ROWS_B, D), bf16),
            pltpu.VMEM((2, ROWS_B, D), bf16),
            dma((4,)),
            dma((MICRO,)), dma((MICRO,)), dma((MICRO,)), dma((MICRO,)),
            dma((MICRO,)), dma((MICRO,)), dma((MICRO,)), dma((MICRO,)),
            dma((NZ,)), dma((NZ * NY,)), dma((NY,)), dma((NZ * NY,)), dma(()), dma((136,)),
            dma((2,)), dma((MICRO,)), dma((MICRO,)), dma((5,)), dma((5,)),
            dma((96,)), dma((NZ,)), dma((NZ * 2,)), dma((2 * NZ,)), dma((2 * NZ,)), dma(()), dma((2,)),
        ],
        compiler_params=pltpu.CompilerParams(
            collective_id=0, has_side_effects=True, vmem_limit_bytes=56 * 2**20
        ),
    )(first_input, upstream, history, example_ids, norm_gain, weight)
    results = (out, scales, weight_grad, gain_grad)
    out, scales, weight_grad, gain_grad = pl.pallas_call(
        hand_over,
        out_shape=tuple(jax.ShapeDtypeStruct(r.shape, r.dtype) for r in results),
        in_specs=[vmem] * 4,
        out_specs=(anywhere,) * 4,
        scratch_shapes=[dma((18,))],
    )(*results)
    return (out[None], scales.T[None], weight_grad[None], gain_grad)


def solution(mesh):
    return jax.shard_map(
        body,
        mesh=mesh,
        in_specs=(
            P("dp", None),
            P("dp", None),
            P("section", None, "dp", None, None),
            P("dp", None),
            P("section", None),
            P("section", "dp", None),
        ),
        out_specs=(
            P("section", "dp", None),
            P("section", "dp", None),
            P("section", "dp", None),
            P("section", None),
        ),
        check_vma=False,
    )
```

```python
import functools

import jax
import jax.numpy as jnp
from jax import lax
from jax.experimental import pallas as pl
from jax.experimental.pallas import tpu as pltpu
from jax.sharding import PartitionSpec as P

MESH = pl.DeviceIdType.MESH
D = 2048
TOK = 256
SEQ = 64
BLOCK = 128
N_SECTION = 8
NZ = 4
NY = 4
SHARD = 64
ROWS_A = 48
ROWS_B = SHARD - ROWS_A
MICRO = 16
MR = TOK // MICRO
WIDE = 32
HALF = D // 2
LAST = N_SECTION - 1
NEAR, OVER = 3, 4
LEAD_0 = 13
LEAD_7 = 16
BACK_0 = 16
BACK_7 = 0
COLS = 512
SENT = 1024
bf16 = jnp.bfloat16
f32 = jnp.float32


def relay_kernel(
    first_hbm, up_hbm, hist_hbm, ids, gain, w_hbm,
    out, scales, weight_grad, gain_out,
    shards, weight_t, hist, x_in, g_in, x_out, g_out, f_relay, b_relay, factor, normed, inv_buf, du_buf, scale_buf, gain_acc, gain_buf,
    pack, pack_out, dmixed, part_a, part_b, y_far_in, y_in, z_in, zb_in, yb_far_in, yb_in,
    local_sem, f_send, f_recv, b_send, b_recv, rf_send, rf_recv, rb_send, rb_recv,
    za_recv, ya_recv, yb_recv, zb_recv, pair_recv, ag_send,
    pack_sems, dz_send, dz_recv, gain_send, gain_recv,
    rs_send, far_recv, ring_recv, line_recv, lineb_recv, farb_recv, ringb_recv,
):
    dp = lax.axis_index("dp")
    s = lax.axis_index("section")
    zl = dp // 8
    y = lax.rem(dp // 2, NY)
    c = lax.rem(dp, 2)

    def device(zl_, y_, c_):
        return (zl_ * 8 + y_ * 2 + c_, s)

    def at_section(s_):
        return (dp, s_)

    y_up, y_dn, y_far = lax.rem(y + 1, NY), lax.rem(y + 3, NY), lax.rem(y + 2, NY)
    partner = device(zl, y, 1 - c)
    prev_dev, next_dev = at_section(lax.rem(s + 7, 8)), at_section(lax.rem(s + 1, 8))
    is_first, is_last = s == 0, s == LAST
    has_prev, has_next = s > 0, s < LAST
    direct_prev = jnp.logical_and(has_prev, s != OVER)
    direct_next = jnp.logical_and(has_next, s != NEAR)

    def z_dev(step):
        return device(lax.rem(zl + step + NZ, NZ), y, c)

    weight = shards.reshape(D, D)

    own_rows = shards.at[zl, y, c]
    load_w = pltpu.make_async_copy(w_hbm.at[0], own_rows, local_sem.at[0])
    load_w.start()
    load_hist = pltpu.make_async_copy(hist_hbm.at[0, 0], hist, local_sem.at[1])
    load_hist.start()
    load_first = pltpu.make_async_copy(first_hbm, x_in, local_sem.at[2])
    load_up = pltpu.make_async_copy(up_hbm, g_in, local_sem.at[3])
    pl.when(is_first)(load_first.start)
    pl.when(is_last)(load_up.start)

    barrier = pltpu.get_barrier_semaphore()
    z_skip = device(lax.rem(zl + 2, NZ), y, c)
    for dev in (partner, device(zl, y_up, c), device(zl, y_dn, c), device(zl, y_far, c), z_skip):
        pl.semaphore_signal(barrier, inc=1, device_id=dev, device_id_type=MESH)
    ends = jnp.logical_or(is_first, is_last)
    middle = jnp.logical_or(s == NEAR, s == OVER)
    others = (
        (z_dev(-1), zl > 0), (z_dev(1), zl < NZ - 1), (prev_dev, direct_prev), (next_dev, direct_next),
        (at_section(NEAR), ends), (at_section(OVER), ends), (at_section(0), middle), (at_section(LAST), middle),
    )
    greeted = jnp.int32(5)
    for dev, there in others:
        greeted = greeted + there.astype(jnp.int32)

        @pl.when(there)
        def _():
            pl.semaphore_signal(barrier, inc=1, device_id=dev, device_id_type=MESH)

    pl.semaphore_wait(barrier, greeted)
    load_w.wait()

    sends = []

    def piece_a(zl_, y_):
        return shards.at[zl_, y_, c, pl.ds(0, ROWS_A)]

    def piece_b(zl_, y_):
        return shards.at[zl_, y_, c, pl.ds(ROWS_A, ROWS_B)]

    def send(ref, recv_sem, dev, cond):
        copy = pltpu.make_async_remote_copy(
            src_ref=ref, dst_ref=ref, send_sem=ag_send.at[len(sends)], recv_sem=recv_sem,
            device_id=dev, device_id_type=MESH,
        )
        sends.append((copy, cond))
        if cond is None:
            copy.start()
        else:
            pl.when(cond)(copy.start)

    def arrived(ref, recv_sem, cond):
        copy = pltpu.make_async_remote_copy(
            src_ref=ref, dst_ref=ref, send_sem=ag_send.at[0], recv_sem=recv_sem,
            device_id=partner, device_id_type=MESH,
        )
        if cond is None:
            copy.wait_recv()
        else:
            pl.when(cond)(copy.wait_recv)

    def both(a, b):
        return b if a is None else jnp.logical_and(a, b)

    def in_line(z_):
        return jnp.logical_and(z_ >= 0, z_ < NZ)

    def origins(distance):
        if distance == 0:
            return [(0, zl, None)]
        if not 0 < distance < NZ:
            return []
        return [(sign, lax.rem(zl + sign * distance + 2 * NZ, NZ), in_line(zl + sign * distance)) for sign in (-1, 1)]

    def even(v):
        return lax.rem(v, 2) == 0

    def odd(v):
        return lax.rem(v, 2) == 1

    def spread_b(y_):
        for sign in (1, -1):
            send(piece_b(zl, y_), zb_recv.at[zl * NY + y_], z_dev(sign), in_line(zl + sign))

    ring_sides = ((y_dn, y_up, even), (y_up, y_dn, odd))
    for sign in (1, -1):
        send(piece_a(zl, y), za_recv.at[zl], z_dev(sign), in_line(zl + sign))
    spread_b(y)
    for y_ in (y_up, y_dn):
        send(piece_b(zl, y), yb_recv.at[y], device(zl, y_, c), None)
    for y_ in (y_up, y_dn):
        send(piece_a(zl, y), ya_recv.at[zl * NY + y], device(zl, y_, c), None)
    send(own_rows, pair_recv, partner, None)

    def line_a(distance):
        for sign, o, there in origins(distance):
            arrived(piece_a(o, y), za_recv.at[o], there)
            send(piece_a(o, y), za_recv.at[o], z_dev(-sign), both(there, in_line(zl - sign)))
            for y_ in (y_up, y_dn):
                send(piece_a(o, y), ya_recv.at[o * NY + y], device(zl, y_, c), there)
            send(piece_a(o, y), pair_recv, partner, there)

    def ring_a(distance):
        for sign, o, there in origins(distance):
            for y_from, y_to, turn in ring_sides:
                arrived(piece_a(o, y_from), ya_recv.at[o * NY + y_from], there)
                send(piece_a(o, y_from), ya_recv.at[o * NY + y_from], device(zl, y_to, c), both(there, turn(o)))
                send(piece_a(o, y_from), pair_recv, partner, there)

    def far_a(distance):
        for sign, o, there in origins(distance):
            arrived(piece_a(o, y_far), ya_recv.at[o * NY + y_far], there)
            send(piece_a(o, y_far), pair_recv, partner, there)

    def ring_b():
        for y_from, y_to, turn in ring_sides:
            arrived(piece_b(zl, y_from), yb_recv.at[y_from], None)
            send(piece_b(zl, y_from), yb_recv.at[y_from], device(zl, y_to, c), turn(zl))
            spread_b(y_from)
            send(piece_b(zl, y_from), pair_recv, partner, None)

    def far_b():
        arrived(piece_b(zl, y_far), yb_recv.at[y_far], None)
        spread_b(y_far)
        send(piece_b(zl, y_far), pair_recv, partner, None)

    def line_b(distance):
        for sign, o, there in origins(distance):
            for y_ in (y, y_dn, y_up, y_far):
                arrived(piece_b(o, y_), zb_recv.at[o * NY + y_], there)
                send(piece_b(o, y_), zb_recv.at[o * NY + y_], z_dev(-sign), both(there, in_line(zl - sign)))
                send(piece_b(o, y_), pair_recv, partner, there)

    line_a(1)
    ring_b()
    line_a(2)
    far_b()
    ring_a(0)
    ring_a(1)
    line_a(3)
    line_b(1)
    ring_a(2)
    ring_a(3)
    line_b(2)
    far_a(2)
    line_b(3)
    far_a(1)
    far_a(0)
    far_a(3)
    arrived(shards.at[pl.ds(0, NZ), pl.ds(0, NY), 1 - c], pair_recv, None)

    load_hist.wait()
    pl.when(is_first)(load_first.wait)
    pl.when(is_last)(load_up.wait)
    gain_acc[...] = jnp.zeros_like(gain_acc)

    def remote(src_ref, dst_ref, send_sem, recv_sem, dev):
        return pltpu.make_async_remote_copy(
            src_ref=src_ref, dst_ref=dst_ref, send_sem=send_sem, recv_sem=recv_sem,
            device_id=dev, device_id_type=MESH,
        )

    def rms(x):
        return lax.rsqrt(jnp.mean(x * x, axis=-1, keepdims=True) + 1e-05)

    def coded(v):
        scale = (jnp.max(jnp.abs(v), axis=-1, keepdims=True) + 1e-06).astype(bf16).astype(f32)
        return (v * (1.0 / scale)).astype(bf16).astype(f32) * scale, scale

    def rows_at(m):
        return pl.ds(pl.multiple_of(m * MR, MR), MR)

    every, low, high = pl.ds(0, D), pl.ds(0, HALF), pl.ds(HALF, HALF)

    def forward_rows(m, size, route):
        rows = pl.ds(pl.multiple_of(m * MR, MR), size)

        @pl.when(has_prev)
        def _():
            for k in range(size // MR):
                part = rows_at(m + k)
                remote(x_out.at[part], x_in.at[part], f_send.at[m + k], f_recv.at[m + k], prev_dev).wait_recv()

        x = x_in[rows, :].astype(f32)
        inverse = rms(x)
        inv_buf[rows, :] = jnp.broadcast_to(inverse, (size, BLOCK))
        nrm = (x * inverse * gain[...]).astype(bf16)
        normed[rows, :] = nrm
        slot = ids[0, m * MR // SEQ]
        old_rows = pl.ds(pl.multiple_of(lax.rem(m * MR, SEQ), MR), size)
        lane = lax.broadcasted_iota(jnp.int32, (size, BLOCK), 1)
        scale_rows = jnp.zeros((size, BLOCK), f32)

        def mixed(n):
            return jnp.dot(nrm, weight[:, n * COLS : (n + 1) * COLS], preferred_element_type=f32)

        ahead = mixed(0)
        for n in range(D // COLS):
            cols = slice(n * COLS, (n + 1) * COLS)
            z = ahead
            if n + 1 < D // COLS:
                ahead = mixed(n + 1)
            sig = 0.5 + 0.5 * jnp.tanh(0.5 * z)
            factor[rows, cols] = sig * (1.0 + z * (1.0 - sig))
            res = (x_in[rows, cols].astype(f32) + z * sig).astype(bf16)
            out[rows, cols] = res
            old = hist[slot, old_rows, cols].astype(f32)
            delta = res.astype(f32) - old
            for b in range(COLS // BLOCK):
                part = slice(b * BLOCK, (b + 1) * BLOCK)
                decoded, scale = coded(delta[:, part])
                scale_rows = jnp.where(lane == n * (COLS // BLOCK) + b, scale, scale_rows)
                if route is not None:
                    x_out[rows, n * COLS + b * BLOCK : n * COLS + (b + 1) * BLOCK] = (old[:, part] + decoded).astype(bf16)
            if route is not None and (n + 1) * COLS % SENT == 0:
                start = (n + 1) * COLS - SENT
                here = pl.ds(start, SENT)
                if route == "direct":
                    remote(x_out.at[rows, here], x_in.at[rows, here], f_send.at[m], f_recv.at[m], next_dev).start()
                else:
                    via = at_section(0 if start < HALF else LAST)
                    there = pl.ds(start % HALF, SENT)
                    remote(x_out.at[rows, here], f_relay.at[rows, there], f_send.at[m], rf_recv.at[m], via).start()
        scale_buf[rows, :] = scale_rows

    def backward_rows(m, size, route):
        rows = pl.ds(pl.multiple_of(m * MR, MR), size)

        @pl.when(has_next)
        def _():
            for k in range(size // MR):
                part = rows_at(m + k)
                remote(g_out.at[part], g_in.at[part], b_send.at[m + k], b_recv.at[m + k], next_dev).wait_recv()

        g = g_in[rows, :].astype(f32)
        dz = (g * factor[rows, :]).astype(bf16)
        dmixed[rows, :] = dz
        for k in range(size // MR):
            dz_copy(m + k).start()
        inverse = inv_buf[rows, 0:1]
        shared = jnp.zeros((size, BLOCK), f32)
        for n in range(D // COLS):
            cols = slice(n * COLS, (n + 1) * COLS)
            dn = jnp.dot(dz, weight_t[:, cols], preferred_element_type=f32)
            unit = x_in[rows, cols].astype(f32) * inverse
            du = dn * gain[:, cols]
            du_buf[0:size, cols] = du
            prod = du * unit
            for b in range(COLS // BLOCK):
                shared = shared + prod[:, b * BLOCK : (b + 1) * BLOCK]
            prod = dn * unit
            total = prod[0:8]
            for k in range(1, size // 8):
                total = total + prod[8 * k : 8 * k + 8]
            gain_acc[:, cols] += total

        if route is None:
            return
        mean = jnp.sum(shared, axis=-1, keepdims=True) * (1.0 / D)
        for n in range(D // SENT):
            for b in range(SENT // BLOCK):
                part = slice(n * SENT + b * BLOCK, n * SENT + (b + 1) * BLOCK)
                unit = x_in[rows, part].astype(f32) * inverse
                dx = g_in[rows, part].astype(f32) + inverse * (du_buf[0:size, part] - unit * mean)
                decoded, _ = coded(dx)
                g_out[rows, part] = decoded.astype(bf16)
            here = pl.ds(n * SENT, SENT)
            for k in range(size // MR):
                sub = rows_at(m + k)
                if route == "direct":
                    remote(g_out.at[sub, here], g_in.at[sub, here], b_send.at[m + k], b_recv.at[m + k], prev_dev).start()
                else:
                    via = at_section(0 if n * SENT < HALF else LAST)
                    there = pl.ds(n * SENT % HALF, SENT)
                    remote(g_out.at[sub, here], b_relay.at[sub, there], b_send.at[m + k], rb_recv.at[m + k], via).start()

    def dz_copy(m):
        here = rows_at(m)
        there = pl.ds(pl.multiple_of(TOK + m * MR, MR), MR)
        return remote(dmixed.at[here], dmixed.at[there], dz_send.at[m], dz_recv.at[m], partner)

    def relay_forward(m, _):
        rows = rows_at(m)

        def passed(cols):
            return remote(f_relay.at[rows], x_in.at[rows, cols], rf_send.at[m], f_recv.at[m], at_section(OVER))

        remote(f_relay.at[rows], f_relay.at[rows], rf_send.at[m], rf_recv.at[m], at_section(NEAR)).wait_recv()
        pl.when(is_first)(passed(low).start)
        pl.when(is_last)(passed(high).start)
        return 0

    def relay_backward(m, _):
        rows = rows_at(m)

        def passed(cols):
            return remote(b_relay.at[rows], g_in.at[rows, cols], rb_send.at[m], b_recv.at[m], at_section(NEAR))

        remote(b_relay.at[rows], b_relay.at[rows], rb_send.at[m], rb_recv.at[m], at_section(OVER)).wait_recv()
        pl.when(is_first)(passed(low).start)
        pl.when(is_last)(passed(high).start)
        return 0

    def transpose_weight(i, _):
        rows = pl.ds(pl.multiple_of(i * 256, 256), 256)
        for j in range(D // 256):
            weight_t[j * 256 : (j + 1) * 256, rows] = weight[rows, j * 256 : (j + 1) * 256].T
        return 0

    def pack_normed(m, _):
        rows = rows_at(m)
        lane = lax.broadcasted_iota(jnp.int32, (MR, BLOCK), 1)
        for t in range(D // 256):
            a = normed[rows, 256 * t : 256 * t + 128].astype(f32)
            b = normed[rows, 256 * t + 128 : 256 * t + 256].astype(f32)
            zero = jnp.where(lane < SHARD, a, pltpu.roll(b, SHARD, 1))
            one = jnp.where(lane < SHARD, pltpu.roll(a, SHARD, 1), b)
            pack[rows, 128 * t : 128 * t + 128] = jnp.where(c == 0, zero, one).astype(bf16)
            pack_out[rows, 128 * t : 128 * t + 128] = jnp.where(c == 0, one, zero).astype(bf16)
        return 0

    pack_copy = remote(pack_out, pack.at[pl.ds(TOK, TOK)], pack_sems.at[0], pack_sems.at[1], partner)

    def forward_all(route):
        def step(m, _):
            forward_rows(m, MR, route)
            if route == "direct":
                @pl.when(jnp.logical_and(is_first, m >= LEAD_0))
                def _():
                    relay_forward(m - LEAD_0, 0)
            return 0

        lax.fori_loop(0, MICRO, step, 0)

    def backward_all(route):
        def step(m, _):
            backward_rows(m, MR, route)
            if route is None:
                @pl.when(m < MICRO - BACK_0)
                def _():
                    relay_backward(m + BACK_0, 0)
            return 0

        lax.fori_loop(0, MICRO, step, 0)

    def turn_step(i, _):
        forward_rows(i * (WIDE // MR), WIDE, None)

        @pl.when(i < (MICRO - LEAD_7) // 2)
        def _():
            relay_forward(LEAD_7 + 2 * i, 0)

        backward_rows(i * (WIDE // MR), WIDE, "direct")

        @pl.when(i < (MICRO - LEAD_7) // 2)
        def _():
            relay_forward(LEAD_7 + 2 * i + 1, 0)

        @pl.when(i == TOK // WIDE - 2)
        def _():
            lax.fori_loop(0, BACK_7, relay_backward, 0)

        return 0

    def drain_gather():
        for copy, cond in sends:
            if cond is None:
                copy.wait_send()
            else:
                pl.when(cond)(copy.wait_send)

    def drain_forward(m, _):
        rows = rows_at(m)

        @pl.when(has_next)
        def _():
            remote(x_out.at[rows], x_in.at[rows], f_send.at[m], f_recv.at[m], next_dev).wait_send()

        @pl.when(ends)
        def _():
            remote(f_relay.at[rows], f_relay.at[rows], rf_send.at[m], rf_recv.at[m], at_section(OVER)).wait_send()

        return 0

    def drain_backward(m, _):
        rows = rows_at(m)
        dz_copy(m).wait_send()

        @pl.when(has_prev)
        def _():
            remote(g_out.at[rows], g_in.at[rows], b_send.at[m], b_recv.at[m], prev_dev).wait_send()

        @pl.when(ends)
        def _():
            remote(b_relay.at[rows], b_relay.at[rows], rb_send.at[m], rb_recv.at[m], at_section(NEAR)).wait_send()

        return 0

    @pl.when(s >= OVER)
    def _():
        lax.fori_loop(0, D // 256, transpose_weight, 0)
        drain_gather()

    @pl.when(is_last)
    def _():
        lax.fori_loop(0, LEAD_7, relay_forward, 0)
        lax.fori_loop(0, TOK // WIDE, turn_step, 0)
        lax.fori_loop(BACK_7, MICRO, relay_backward, 0)

    @pl.when(direct_next)
    def _():
        forward_all("direct")

    @pl.when(s == NEAR)
    def _():
        forward_all("relay")

    @pl.when(is_first)
    def _():
        lax.fori_loop(MICRO - LEAD_0, MICRO, relay_forward, 0)

    @pl.when(s < OVER)
    def _():
        lax.fori_loop(0, D // 256, transpose_weight, 0)
        lax.fori_loop(0, MICRO, pack_normed, 0)
        pack_copy.start()
        drain_gather()
        lax.fori_loop(0, MICRO, drain_forward, 0)
        scales[...] = scale_buf[...].T[: D // BLOCK].astype(bf16)

    @pl.when(is_first)
    def _():
        lax.fori_loop(0, BACK_0, relay_backward, 0)
        backward_all(None)

    @pl.when(jnp.logical_and(direct_prev, has_next))
    def _():
        backward_all("direct")

    @pl.when(s == OVER)
    def _():
        backward_all("relay")

    @pl.when(s >= OVER)
    def _():
        lax.fori_loop(0, MICRO, pack_normed, 0)
        pack_copy.start()
        scales[...] = scale_buf[...].T[: D // BLOCK].astype(bf16)

    pack_copy.wait_recv()
    for m in range(MICRO):
        dz_copy(m).wait_recv()
    scatter = []

    def hand(src_ref, dst_ref, recv_sem, dev, cond=None):
        copy = remote(src_ref, dst_ref, rs_send.at[len(scatter)], recv_sem, dev)
        scatter.append((copy, cond))
        if cond is None:
            copy.start()
        else:
            pl.when(cond)(copy.start)

    def landed(ref, recv_sem, cond=None):
        copy = remote(ref, ref, rs_send.at[0], recv_sem, partner)
        if cond is None:
            copy.wait_recv()
        else:
            pl.when(cond)(copy.wait_recv)

    def add_to(ref, *terms):
        total = ref[...].astype(f32)
        for term in terms:
            total = total + term[...].astype(f32)
        ref[...] = total.astype(ref.dtype)

    low_half = zl < 2
    order = (
        jnp.where(low_half, 3, 0), jnp.where(low_half, 2, 1), jnp.where(low_half, 1 - zl, 5 - zl), zl,
    )
    up_dev, dn_dev = device(zl, y_up, c), device(zl, y_dn, c)

    def line(k):
        right = order[k] > zl
        upstream = jnp.where(right, zl > 0, zl < NZ - 1)
        return right, upstream, jnp.where(right, 0, 1)

    def b_rows(y_):
        return pl.ds(pl.multiple_of(y_ * ROWS_B, ROWS_B), ROWS_B)

    def send_line_b(k, cond):
        right, _, side = line(k)
        zd = order[k]
        for step, way in ((1, right), (-1, jnp.logical_not(right))):
            hand(part_b.at[zd], zb_in.at[side, zd], lineb_recv.at[side * NZ + zd], z_dev(step), both(cond, way))

    def send_line_a(k, cond):
        right, _, side = line(k)
        zd = order[k]
        for step, way in ((1, right), (-1, jnp.logical_not(right))):
            hand(part_a.at[zd, y], z_in.at[side, zd], line_recv.at[side * NZ + zd], z_dev(step), both(cond, way))

    def pass_line_b(k):
        _, upstream, side = line(k)
        zd = order[k]
        landed(zb_in.at[side, zd], lineb_recv.at[side * NZ + zd], upstream)

        @pl.when(upstream)
        def _():
            add_to(part_b.at[zd], zb_in.at[side, zd])

        send_line_b(k, upstream)

    def own_line_b():
        for side, there in ((0, zl > 0), (1, zl < NZ - 1)):
            landed(zb_in.at[side, zl], lineb_recv.at[side * NZ + zl], there)

            @pl.when(there)
            def _():
                add_to(part_b.at[zl], zb_in.at[side, zl])

        for dev, way in ((up_dev, even(zl)), (dn_dev, odd(zl))):
            hand(part_b.at[zl, b_rows(y_far)], yb_far_in, farb_recv, dev, way)

    def own_line_a():
        for side, there in ((0, zl > 0), (1, zl < NZ - 1)):
            landed(z_in.at[side, zl], line_recv.at[side * NZ + zl], there)

            @pl.when(there)
            def _():
                weight_grad[0:ROWS_A, :] += z_in[side, zl].astype(f32)

    def ring_b_out():
        landed(yb_far_in, farb_recv)
        add_to(part_b.at[zl, b_rows(jnp.where(even(zl), y_up, y_dn))], yb_far_in)
        hand(part_b.at[zl, b_rows(y_up)], yb_in.at[0], ringb_recv.at[0], up_dev)
        hand(part_b.at[zl, b_rows(y_dn)], yb_in.at[1], ringb_recv.at[1], dn_dev)

    def ring_b_in():
        for side in range(2):
            landed(yb_in.at[side], ringb_recv.at[side])
        weight_grad[ROWS_A:SHARD, :] = (
            part_b[zl, b_rows(y)].astype(f32) + yb_in[0].astype(f32) + yb_in[1].astype(f32)
        )

    def pass_line_a(k):
        _, upstream, side = line(k)
        zd = order[k]
        landed(z_in.at[side, zd], line_recv.at[side * NZ + zd], upstream)

        @pl.when(upstream)
        def _():
            add_to(part_a.at[zd, y], z_in.at[side, zd])

        send_line_a(k, upstream)

    def ring_out(k):
        zd = order[k]
        landed(y_far_in.at[zd], far_recv.at[zd])
        target = jnp.where(even(zd), y_up, y_dn)
        add_to(part_a.at[zd, target], y_far_in.at[zd])
        hand(part_a.at[zd, y_up], y_in.at[zd, 0], ring_recv.at[zd * 2], up_dev)
        hand(part_a.at[zd, y_dn], y_in.at[zd, 1], ring_recv.at[zd * 2 + 1], dn_dev)

    def ring_in(k):
        zd = order[k]
        for side in range(2):
            landed(y_in.at[zd, side], ring_recv.at[zd * 2 + side])
        if k < NZ - 1:
            add_to(part_a.at[zd, y], y_in.at[zd, 0], y_in.at[zd, 1])
            send_line_a(k, jnp.logical_not(line(k)[1]))
        else:
            weight_grad[0:ROWS_A, :] = (
                part_a[zd, y].astype(f32) + y_in[zd, 0].astype(f32) + y_in[zd, 1].astype(f32)
            )

    gain_steps = (
        partner, device(zl, jnp.where(even(y), y + 1, y - 1), c), device(zl, y_far, c),
        device(jnp.where(even(zl), zl + 1, zl - 1), y, c), z_skip,
    )
    gain_buf[0] = jnp.sum(gain_acc[...], axis=0, keepdims=True)

    def gain_copy(k):
        return remote(gain_buf.at[k], gain_buf.at[6 + k], gain_send.at[k], gain_recv.at[k], gain_steps[k])

    def gain_add(k):
        gain_copy(k).wait_recv()
        gain_buf[k + 1] = gain_buf[k] + gain_buf[6 + k]
        if k + 1 < len(gain_steps):
            gain_copy(k + 1).start()

    def produce(k):
        zd = order[k]
        cols = pl.ds(pl.multiple_of(zd * 256, 256), 256)
        total = lax.dot_general(pack[:, cols], dmixed[...], (((0,), (0,)), ((), ())), preferred_element_type=f32).astype(bf16)
        for j in range(NY):
            part_a[zd, j] = total[j * SHARD : j * SHARD + ROWS_A]
            part_b[zd, j * ROWS_B : (j + 1) * ROWS_B] = total[j * SHARD + ROWS_A : (j + 1) * SHARD]
        for dev, way in ((up_dev, even(zd)), (dn_dev, odd(zd))):
            hand(part_a.at[zd, y_far], y_far_in.at[zd], far_recv.at[zd], dev, way)
        if k < NZ - 1:
            send_line_b(k, jnp.logical_not(line(k)[1]))

    produce(0)
    gain_copy(0).start()
    produce(1)
    ring_out(0)
    produce(2)
    pass_line_b(0)
    gain_add(0)
    produce(3)
    ring_out(1)
    pass_line_b(1)
    ring_in(0)
    gain_add(1)
    ring_out(2)
    pass_line_b(2)
    ring_in(1)
    gain_add(2)
    pass_line_a(0)
    own_line_b()
    gain_add(3)
    ring_out(3)
    ring_in(2)
    gain_add(4)
    ring_b_out()
    pass_line_a(1)
    before = len(scatter)
    pass_line_a(2)
    last_hops = len(scatter) - before

    def drain_sums(start, stop):
        for copy, cond in scatter[start:stop]:
            if cond is None:
                copy.wait_send()
            else:
                pl.when(cond)(copy.wait_send)

    ring_in(3)
    ring_b_in()
    lax.fori_loop(0, MICRO, drain_backward, 0)
    pack_copy.wait_send()
    for k in range(len(gain_steps)):
        gain_copy(k).wait_send()
    drain_sums(0, before)
    own_line_a()

    gain_out[...] = gain_buf[5]

    drain_sums(len(scatter) - last_hops, len(scatter))

    @pl.when(s >= OVER)
    def _():
        lax.fori_loop(0, MICRO, drain_forward, 0)


def hand_over(*refs):
    n = len(refs) // 2
    copies = []
    for src, dst in zip(refs[:n], refs[n : 2 * n]):
        rows = src.shape[0]
        pieces = 8 if rows * src.shape[1] >= 2**17 else 1
        for k in range(pieces):
            part = pl.ds(k * (rows // pieces), rows // pieces)
            copies.append(pltpu.make_async_copy(src.at[part], dst.at[part], refs[-1].at[len(copies)]))
    for copy in copies:
        copy.start()
    for copy in copies:
        copy.wait()


def body(first_input, upstream, history, example_ids, norm_gain, weight):
    vmem = pl.BlockSpec(memory_space=pltpu.VMEM)
    anywhere = pl.BlockSpec(memory_space=pl.ANY)
    smem = pl.BlockSpec(memory_space=pltpu.SMEM)
    dma = pltpu.SemaphoreType.DMA
    out, scales, weight_grad, gain_grad = pl.pallas_call(
        relay_kernel,
        out_shape=(
            jax.ShapeDtypeStruct((TOK, D), bf16),
            jax.ShapeDtypeStruct((D // BLOCK, TOK), bf16),
            jax.ShapeDtypeStruct((SHARD, D), f32),
            jax.ShapeDtypeStruct((1, D), f32),
        ),
        in_specs=[anywhere, anywhere, anywhere, smem, vmem, anywhere],
        out_specs=(vmem,) * 4,
        scratch_shapes=[
            pltpu.VMEM((NZ, NY, 2, SHARD, D), bf16),
            pltpu.VMEM((D, D), bf16),
            pltpu.VMEM((4, SEQ, D), bf16),
            pltpu.VMEM((TOK, D), bf16),
            pltpu.VMEM((TOK, D), bf16),
            pltpu.VMEM((TOK, D), bf16),
            pltpu.VMEM((TOK, D), bf16),
            pltpu.VMEM((TOK, HALF), bf16),
            pltpu.VMEM((TOK, HALF), bf16),
            pltpu.VMEM((TOK, D), f32),
            pltpu.VMEM((TOK, D), bf16),
            pltpu.VMEM((TOK, BLOCK), f32),
            pltpu.VMEM((WIDE, D), f32),
            pltpu.VMEM((TOK, BLOCK), f32),
            pltpu.VMEM((8, D), f32),
            pltpu.VMEM((11, 1, D), f32),
            pltpu.VMEM((2 * TOK, HALF), bf16),
            pltpu.VMEM((TOK, HALF), bf16),
            pltpu.VMEM((2 * TOK, D), bf16),
            pltpu.VMEM((NZ, NY, ROWS_A, D), bf16),
            pltpu.VMEM((NZ, NY * ROWS_B, D), bf16),
            pltpu.VMEM((NZ, ROWS_A, D), bf16),
            pltpu.VMEM((NZ, 2, ROWS_A, D), bf16),
            pltpu.VMEM((2, NZ, ROWS_A, D), bf16),
            pltpu.VMEM((2, NZ, NY * ROWS_B, D), bf16),
            pltpu.VMEM((ROWS_B, D), bf16),
            pltpu.VMEM((2, ROWS_B, D), bf16),
            dma((4,)),
            dma((MICRO,)), dma((MICRO,)), dma((MICRO,)), dma((MICRO,)),
            dma((MICRO,)), dma((MICRO,)), dma((MICRO,)), dma((MICRO,)),
            dma((NZ,)), dma((NZ * NY,)), dma((NY,)), dma((NZ * NY,)), dma(()), dma((136,)),
            dma((2,)), dma((MICRO,)), dma((MICRO,)), dma((5,)), dma((5,)),
            dma((96,)), dma((NZ,)), dma((NZ * 2,)), dma((2 * NZ,)), dma((2 * NZ,)), dma(()), dma((2,)),
        ],
        compiler_params=pltpu.CompilerParams(
            collective_id=0, has_side_effects=True, vmem_limit_bytes=56 * 2**20
        ),
    )(first_input, upstream, history, example_ids, norm_gain, weight)
    results = (out, scales, weight_grad, gain_grad)
    out, scales, weight_grad, gain_grad = pl.pallas_call(
        hand_over,
        out_shape=tuple(jax.ShapeDtypeStruct(r.shape, r.dtype) for r in results),
        in_specs=[vmem] * 4,
        out_specs=(anywhere,) * 4,
        scratch_shapes=[dma((18,))],
    )(*results)
    return (out[None], scales.T[None], weight_grad[None], gain_grad)


def solution(mesh):
    return jax.shard_map(
        body,
        mesh=mesh,
        in_specs=(
            P("dp", None),
            P("dp", None),
            P("section", None, "dp", None, None),
            P("dp", None),
            P("section", None),
            P("section", "dp", None),
        ),
        out_specs=(
            P("section", "dp", None),
            P("section", "dp", None),
            P("section", "dp", None),
            P("section", None),
        ),
        check_vma=False,
    )
```

```python
import functools

import jax
import jax.numpy as jnp
from jax import lax
from jax.experimental import pallas as pl
from jax.experimental.pallas import tpu as pltpu
from jax.sharding import PartitionSpec as P

MESH = pl.DeviceIdType.MESH
D = 2048
TOK = 256
SEQ = 64
BLOCK = 128
N_SECTION = 8
NZ = 4
NY = 4
SHARD = 64
ROWS_A = 48
ROWS_B = SHARD - ROWS_A
MICRO = 16
MR = TOK // MICRO
WIDE = 32
HALF = D // 2
LAST = N_SECTION - 1
NEAR, OVER = 3, 4
LEAD_0 = 13
LEAD_7 = 14
BACK_0 = 16
BACK_7 = 0
COLS = 512
SENT = 1024
bf16 = jnp.bfloat16
f32 = jnp.float32


def relay_kernel(
    first_hbm, up_hbm, hist_hbm, ids, gain, w_hbm,
    out, scales, weight_grad, gain_out,
    shards, weight_t, hist, x_in, g_in, x_out, g_out, f_relay, b_relay, factor, normed, inv_buf, du_buf, scale_buf, gain_acc, gain_buf,
    pack, pack_out, dmixed, part_a, part_b, y_far_in, y_in, z_in, zb_in, yb_far_in, yb_in,
    local_sem, f_send, f_recv, b_send, b_recv, rf_send, rf_recv, rb_send, rb_recv,
    za_recv, ya_recv, yb_recv, zb_recv, pair_recv, ag_send,
    pack_sems, dz_send, dz_recv, gain_send, gain_recv,
    rs_send, far_recv, ring_recv, line_recv, lineb_recv, farb_recv, ringb_recv,
):
    dp = lax.axis_index("dp")
    s = lax.axis_index("section")
    zl = dp // 8
    y = lax.rem(dp // 2, NY)
    c = lax.rem(dp, 2)

    def device(zl_, y_, c_):
        return (zl_ * 8 + y_ * 2 + c_, s)

    def at_section(s_):
        return (dp, s_)

    y_up, y_dn, y_far = lax.rem(y + 1, NY), lax.rem(y + 3, NY), lax.rem(y + 2, NY)
    partner = device(zl, y, 1 - c)
    prev_dev, next_dev = at_section(lax.rem(s + 7, 8)), at_section(lax.rem(s + 1, 8))
    is_first, is_last = s == 0, s == LAST
    has_prev, has_next = s > 0, s < LAST
    direct_prev = jnp.logical_and(has_prev, s != OVER)
    direct_next = jnp.logical_and(has_next, s != NEAR)

    def z_dev(step):
        return device(lax.rem(zl + step + NZ, NZ), y, c)

    weight = shards.reshape(D, D)

    own_rows = shards.at[zl, y, c]
    load_w = pltpu.make_async_copy(w_hbm.at[0], own_rows, local_sem.at[0])
    load_w.start()
    load_hist = pltpu.make_async_copy(hist_hbm.at[0, 0], hist, local_sem.at[1])
    load_hist.start()
    load_first = pltpu.make_async_copy(first_hbm, x_in, local_sem.at[2])
    load_up = pltpu.make_async_copy(up_hbm, g_in, local_sem.at[3])
    pl.when(is_first)(load_first.start)
    pl.when(is_last)(load_up.start)

    barrier = pltpu.get_barrier_semaphore()
    z_skip = device(lax.rem(zl + 2, NZ), y, c)
    for dev in (partner, device(zl, y_up, c), device(zl, y_dn, c), device(zl, y_far, c), z_skip):
        pl.semaphore_signal(barrier, inc=1, device_id=dev, device_id_type=MESH)
    ends = jnp.logical_or(is_first, is_last)
    middle = jnp.logical_or(s == NEAR, s == OVER)
    others = (
        (z_dev(-1), zl > 0), (z_dev(1), zl < NZ - 1), (prev_dev, direct_prev), (next_dev, direct_next),
        (at_section(NEAR), ends), (at_section(OVER), ends), (at_section(0), middle), (at_section(LAST), middle),
    )
    greeted = jnp.int32(5)
    for dev, there in others:
        greeted = greeted + there.astype(jnp.int32)

        @pl.when(there)
        def _():
            pl.semaphore_signal(barrier, inc=1, device_id=dev, device_id_type=MESH)

    pl.semaphore_wait(barrier, greeted)
    load_w.wait()

    sends = []

    def piece_a(zl_, y_):
        return shards.at[zl_, y_, c, pl.ds(0, ROWS_A)]

    def piece_b(zl_, y_):
        return shards.at[zl_, y_, c, pl.ds(ROWS_A, ROWS_B)]

    def send(ref, recv_sem, dev, cond):
        copy = pltpu.make_async_remote_copy(
            src_ref=ref, dst_ref=ref, send_sem=ag_send.at[len(sends)], recv_sem=recv_sem,
            device_id=dev, device_id_type=MESH,
        )
        sends.append((copy, cond))
        if cond is None:
            copy.start()
        else:
            pl.when(cond)(copy.start)

    def arrived(ref, recv_sem, cond):
        copy = pltpu.make_async_remote_copy(
            src_ref=ref, dst_ref=ref, send_sem=ag_send.at[0], recv_sem=recv_sem,
            device_id=partner, device_id_type=MESH,
        )
        if cond is None:
            copy.wait_recv()
        else:
            pl.when(cond)(copy.wait_recv)

    def both(a, b):
        return b if a is None else jnp.logical_and(a, b)

    def in_line(z_):
        return jnp.logical_and(z_ >= 0, z_ < NZ)

    def origins(distance):
        if distance == 0:
            return [(0, zl, None)]
        if not 0 < distance < NZ:
            return []
        return [(sign, lax.rem(zl + sign * distance + 2 * NZ, NZ), in_line(zl + sign * distance)) for sign in (-1, 1)]

    def even(v):
        return lax.rem(v, 2) == 0

    def odd(v):
        return lax.rem(v, 2) == 1

    def spread_b(y_):
        for sign in (1, -1):
            send(piece_b(zl, y_), zb_recv.at[zl * NY + y_], z_dev(sign), in_line(zl + sign))

    ring_sides = ((y_dn, y_up, even), (y_up, y_dn, odd))
    for sign in (1, -1):
        send(piece_a(zl, y), za_recv.at[zl], z_dev(sign), in_line(zl + sign))
    spread_b(y)
    for y_ in (y_up, y_dn):
        send(piece_b(zl, y), yb_recv.at[y], device(zl, y_, c), None)
    for y_ in (y_up, y_dn):
        send(piece_a(zl, y), ya_recv.at[zl * NY + y], device(zl, y_, c), None)
    send(own_rows, pair_recv, partner, None)

    def line_a(distance):
        for sign, o, there in origins(distance):
            arrived(piece_a(o, y), za_recv.at[o], there)
            send(piece_a(o, y), za_recv.at[o], z_dev(-sign), both(there, in_line(zl - sign)))
            for y_ in (y_up, y_dn):
                send(piece_a(o, y), ya_recv.at[o * NY + y], device(zl, y_, c), there)
            send(piece_a(o, y), pair_recv, partner, there)

    def ring_a(distance):
        for sign, o, there in origins(distance):
            for y_from, y_to, turn in ring_sides:
                arrived(piece_a(o, y_from), ya_recv.at[o * NY + y_from], there)
                send(piece_a(o, y_from), ya_recv.at[o * NY + y_from], device(zl, y_to, c), both(there, turn(o)))
                send(piece_a(o, y_from), pair_recv, partner, there)

    def far_a(distance):
        for sign, o, there in origins(distance):
            arrived(piece_a(o, y_far), ya_recv.at[o * NY + y_far], there)
            send(piece_a(o, y_far), pair_recv, partner, there)

    def ring_b():
        for y_from, y_to, turn in ring_sides:
            arrived(piece_b(zl, y_from), yb_recv.at[y_from], None)
            send(piece_b(zl, y_from), yb_recv.at[y_from], device(zl, y_to, c), turn(zl))
            spread_b(y_from)
            send(piece_b(zl, y_from), pair_recv, partner, None)

    def far_b():
        arrived(piece_b(zl, y_far), yb_recv.at[y_far], None)
        spread_b(y_far)
        send(piece_b(zl, y_far), pair_recv, partner, None)

    def line_b(distance):
        for sign, o, there in origins(distance):
            for y_ in (y, y_dn, y_up, y_far):
                arrived(piece_b(o, y_), zb_recv.at[o * NY + y_], there)
                send(piece_b(o, y_), zb_recv.at[o * NY + y_], z_dev(-sign), both(there, in_line(zl - sign)))
                send(piece_b(o, y_), pair_recv, partner, there)

    line_a(1)
    ring_b()
    line_a(2)
    far_b()
    ring_a(0)
    ring_a(1)
    line_a(3)
    line_b(1)
    ring_a(2)
    ring_a(3)
    line_b(2)
    far_a(2)
    line_b(3)
    far_a(1)
    far_a(0)
    far_a(3)
    arrived(shards.at[pl.ds(0, NZ), pl.ds(0, NY), 1 - c], pair_recv, None)

    load_hist.wait()
    pl.when(is_first)(load_first.wait)
    pl.when(is_last)(load_up.wait)
    gain_acc[...] = jnp.zeros_like(gain_acc)

    def remote(src_ref, dst_ref, send_sem, recv_sem, dev):
        return pltpu.make_async_remote_copy(
            src_ref=src_ref, dst_ref=dst_ref, send_sem=send_sem, recv_sem=recv_sem,
            device_id=dev, device_id_type=MESH,
        )

    def rms(x):
        return lax.rsqrt(jnp.mean(x * x, axis=-1, keepdims=True) + 1e-05)

    def coded(v):
        scale = (jnp.max(jnp.abs(v), axis=-1, keepdims=True) + 1e-06).astype(bf16).astype(f32)
        return (v * (1.0 / scale)).astype(bf16).astype(f32) * scale, scale

    def rows_at(m):
        return pl.ds(pl.multiple_of(m * MR, MR), MR)

    every, low, high = pl.ds(0, D), pl.ds(0, HALF), pl.ds(HALF, HALF)

    def forward_rows(m, size, route):
        rows = pl.ds(pl.multiple_of(m * MR, MR), size)

        @pl.when(has_prev)
        def _():
            for k in range(size // MR):
                part = rows_at(m + k)
                remote(x_out.at[part], x_in.at[part], f_send.at[m + k], f_recv.at[m + k], prev_dev).wait_recv()

        x = x_in[rows, :].astype(f32)
        inverse = rms(x)
        inv_buf[rows, :] = jnp.broadcast_to(inverse, (size, BLOCK))
        nrm = (x * inverse * gain[...]).astype(bf16)
        normed[rows, :] = nrm
        slot = ids[0, m * MR // SEQ]
        old_rows = pl.ds(pl.multiple_of(lax.rem(m * MR, SEQ), MR), size)
        lane = lax.broadcasted_iota(jnp.int32, (size, BLOCK), 1)
        scale_rows = jnp.zeros((size, BLOCK), f32)

        def mixed(n):
            return jnp.dot(nrm, weight[:, n * COLS : (n + 1) * COLS], preferred_element_type=f32)

        ahead = mixed(0)
        for n in range(D // COLS):
            cols = slice(n * COLS, (n + 1) * COLS)
            z = ahead
            if n + 1 < D // COLS:
                ahead = mixed(n + 1)
            sig = 0.5 + 0.5 * jnp.tanh(0.5 * z)
            factor[rows, cols] = sig * (1.0 + z * (1.0 - sig))
            res = (x_in[rows, cols].astype(f32) + z * sig).astype(bf16)
            out[rows, cols] = res
            old = hist[slot, old_rows, cols].astype(f32)
            delta = res.astype(f32) - old
            for b in range(COLS // BLOCK):
                part = slice(b * BLOCK, (b + 1) * BLOCK)
                decoded, scale = coded(delta[:, part])
                scale_rows = jnp.where(lane == n * (COLS // BLOCK) + b, scale, scale_rows)
                if route is not None:
                    x_out[rows, n * COLS + b * BLOCK : n * COLS + (b + 1) * BLOCK] = (old[:, part] + decoded).astype(bf16)
            if route is not None and (n + 1) * COLS % SENT == 0:
                start = (n + 1) * COLS - SENT
                here = pl.ds(start, SENT)
                if route == "direct":
                    remote(x_out.at[rows, here], x_in.at[rows, here], f_send.at[m], f_recv.at[m], next_dev).start()
                else:
                    via = at_section(0 if start < HALF else LAST)
                    there = pl.ds(start % HALF, SENT)
                    remote(x_out.at[rows, here], f_relay.at[rows, there], f_send.at[m], rf_recv.at[m], via).start()
        scale_buf[rows, :] = scale_rows

    def backward_rows(m, size, route):
        rows = pl.ds(pl.multiple_of(m * MR, MR), size)

        @pl.when(has_next)
        def _():
            for k in range(size // MR):
                part = rows_at(m + k)
                remote(g_out.at[part], g_in.at[part], b_send.at[m + k], b_recv.at[m + k], next_dev).wait_recv()

        g = g_in[rows, :].astype(f32)
        dz = (g * factor[rows, :]).astype(bf16)
        dmixed[rows, :] = dz
        for k in range(size // MR):
            dz_copy(m + k).start()
        inverse = inv_buf[rows, 0:1]
        shared = jnp.zeros((size, BLOCK), f32)
        for n in range(D // COLS):
            cols = slice(n * COLS, (n + 1) * COLS)
            dn = jnp.dot(dz, weight_t[:, cols], preferred_element_type=f32)
            unit = x_in[rows, cols].astype(f32) * inverse
            du = dn * gain[:, cols]
            du_buf[0:size, cols] = du
            prod = du * unit
            for b in range(COLS // BLOCK):
                shared = shared + prod[:, b * BLOCK : (b + 1) * BLOCK]
            prod = dn * unit
            total = prod[0:8]
            for k in range(1, size // 8):
                total = total + prod[8 * k : 8 * k + 8]
            gain_acc[:, cols] += total

        if route is None:
            return
        mean = jnp.sum(shared, axis=-1, keepdims=True) * (1.0 / D)
        for n in range(D // SENT):
            for b in range(SENT // BLOCK):
                part = slice(n * SENT + b * BLOCK, n * SENT + (b + 1) * BLOCK)
                unit = x_in[rows, part].astype(f32) * inverse
                dx = g_in[rows, part].astype(f32) + inverse * (du_buf[0:size, part] - unit * mean)
                decoded, _ = coded(dx)
                g_out[rows, part] = decoded.astype(bf16)
            here = pl.ds(n * SENT, SENT)
            for k in range(size // MR):
                sub = rows_at(m + k)
                if route == "direct":
                    remote(g_out.at[sub, here], g_in.at[sub, here], b_send.at[m + k], b_recv.at[m + k], prev_dev).start()
                else:
                    via = at_section(0 if n * SENT < HALF else LAST)
                    there = pl.ds(n * SENT % HALF, SENT)
                    remote(g_out.at[sub, here], b_relay.at[sub, there], b_send.at[m + k], rb_recv.at[m + k], via).start()

    def dz_copy(m):
        here = rows_at(m)
        there = pl.ds(pl.multiple_of(TOK + m * MR, MR), MR)
        return remote(dmixed.at[here], dmixed.at[there], dz_send.at[m], dz_recv.at[m], partner)

    def relay_forward(m, _):
        rows = rows_at(m)

        def passed(cols):
            return remote(f_relay.at[rows], x_in.at[rows, cols], rf_send.at[m], f_recv.at[m], at_section(OVER))

        remote(f_relay.at[rows], f_relay.at[rows], rf_send.at[m], rf_recv.at[m], at_section(NEAR)).wait_recv()
        pl.when(is_first)(passed(low).start)
        pl.when(is_last)(passed(high).start)
        return 0

    def relay_backward(m, _):
        rows = rows_at(m)

        def passed(cols):
            return remote(b_relay.at[rows], g_in.at[rows, cols], rb_send.at[m], b_recv.at[m], at_section(NEAR))

        remote(b_relay.at[rows], b_relay.at[rows], rb_send.at[m], rb_recv.at[m], at_section(OVER)).wait_recv()
        pl.when(is_first)(passed(low).start)
        pl.when(is_last)(passed(high).start)
        return 0

    def transpose_weight(i, _):
        rows = pl.ds(pl.multiple_of(i * 256, 256), 256)
        for j in range(D // 256):
            weight_t[j * 256 : (j + 1) * 256, rows] = weight[rows, j * 256 : (j + 1) * 256].T
        return 0

    def pack_normed(m, _):
        rows = rows_at(m)
        lane = lax.broadcasted_iota(jnp.int32, (MR, BLOCK), 1)
        for t in range(D // 256):
            a = normed[rows, 256 * t : 256 * t + 128].astype(f32)
            b = normed[rows, 256 * t + 128 : 256 * t + 256].astype(f32)
            zero = jnp.where(lane < SHARD, a, pltpu.roll(b, SHARD, 1))
            one = jnp.where(lane < SHARD, pltpu.roll(a, SHARD, 1), b)
            pack[rows, 128 * t : 128 * t + 128] = jnp.where(c == 0, zero, one).astype(bf16)
            pack_out[rows, 128 * t : 128 * t + 128] = jnp.where(c == 0, one, zero).astype(bf16)
        return 0

    pack_copy = remote(pack_out, pack.at[pl.ds(TOK, TOK)], pack_sems.at[0], pack_sems.at[1], partner)

    def forward_all(route):
        def step(m, _):
            forward_rows(m, MR, route)
            if route == "direct":
                @pl.when(jnp.logical_and(is_first, m >= LEAD_0))
                def _():
                    relay_forward(m - LEAD_0, 0)
            return 0

        lax.fori_loop(0, MICRO, step, 0)

    def backward_all(route):
        def step(m, _):
            backward_rows(m, MR, route)
            if route is None:
                @pl.when(m < MICRO - BACK_0)
                def _():
                    relay_backward(m + BACK_0, 0)
            return 0

        lax.fori_loop(0, MICRO, step, 0)

    def turn_step(i, _):
        forward_rows(i * (WIDE // MR), WIDE, None)

        @pl.when(i < (MICRO - LEAD_7) // 2)
        def _():
            relay_forward(LEAD_7 + 2 * i, 0)

        backward_rows(i * (WIDE // MR), WIDE, "direct")

        @pl.when(i < (MICRO - LEAD_7) // 2)
        def _():
            relay_forward(LEAD_7 + 2 * i + 1, 0)

        @pl.when(i == TOK // WIDE - 2)
        def _():
            lax.fori_loop(0, BACK_7, relay_backward, 0)

        return 0

    def drain_gather():
        for copy, cond in sends:
            if cond is None:
                copy.wait_send()
            else:
                pl.when(cond)(copy.wait_send)

    def drain_forward(m, _):
        rows = rows_at(m)

        @pl.when(has_next)
        def _():
            remote(x_out.at[rows], x_in.at[rows], f_send.at[m], f_recv.at[m], next_dev).wait_send()

        @pl.when(ends)
        def _():
            remote(f_relay.at[rows], f_relay.at[rows], rf_send.at[m], rf_recv.at[m], at_section(OVER)).wait_send()

        return 0

    def drain_backward(m, _):
        rows = rows_at(m)
        dz_copy(m).wait_send()

        @pl.when(has_prev)
        def _():
            remote(g_out.at[rows], g_in.at[rows], b_send.at[m], b_recv.at[m], prev_dev).wait_send()

        @pl.when(ends)
        def _():
            remote(b_relay.at[rows], b_relay.at[rows], rb_send.at[m], rb_recv.at[m], at_section(NEAR)).wait_send()

        return 0

    @pl.when(s >= OVER)
    def _():
        lax.fori_loop(0, D // 256, transpose_weight, 0)
        drain_gather()

    @pl.when(is_last)
    def _():
        lax.fori_loop(0, LEAD_7, relay_forward, 0)
        lax.fori_loop(0, TOK // WIDE, turn_step, 0)
        lax.fori_loop(BACK_7, MICRO, relay_backward, 0)

    @pl.when(direct_next)
    def _():
        forward_all("direct")

    @pl.when(s == NEAR)
    def _():
        forward_all("relay")

    @pl.when(is_first)
    def _():
        lax.fori_loop(MICRO - LEAD_0, MICRO, relay_forward, 0)

    @pl.when(s < OVER)
    def _():
        lax.fori_loop(0, D // 256, transpose_weight, 0)
        lax.fori_loop(0, MICRO, pack_normed, 0)
        pack_copy.start()
        drain_gather()
        lax.fori_loop(0, MICRO, drain_forward, 0)
        scales[...] = scale_buf[...].T[: D // BLOCK].astype(bf16)

    @pl.when(is_first)
    def _():
        lax.fori_loop(0, BACK_0, relay_backward, 0)
        backward_all(None)

    @pl.when(jnp.logical_and(direct_prev, has_next))
    def _():
        backward_all("direct")

    @pl.when(s == OVER)
    def _():
        backward_all("relay")

    @pl.when(s >= OVER)
    def _():
        lax.fori_loop(0, MICRO, pack_normed, 0)
        pack_copy.start()
        scales[...] = scale_buf[...].T[: D // BLOCK].astype(bf16)

    pack_copy.wait_recv()
    for m in range(MICRO):
        dz_copy(m).wait_recv()
    scatter = []

    def hand(src_ref, dst_ref, recv_sem, dev, cond=None):
        copy = remote(src_ref, dst_ref, rs_send.at[len(scatter)], recv_sem, dev)
        scatter.append((copy, cond))
        if cond is None:
            copy.start()
        else:
            pl.when(cond)(copy.start)

    def landed(ref, recv_sem, cond=None):
        copy = remote(ref, ref, rs_send.at[0], recv_sem, partner)
        if cond is None:
            copy.wait_recv()
        else:
            pl.when(cond)(copy.wait_recv)

    def add_to(ref, *terms):
        total = ref[...].astype(f32)
        for term in terms:
            total = total + term[...].astype(f32)
        ref[...] = total.astype(ref.dtype)

    low_half = zl < 2
    order = (
        jnp.where(low_half, 3, 0), jnp.where(low_half, 2, 1), jnp.where(low_half, 1 - zl, 5 - zl), zl,
    )
    up_dev, dn_dev = device(zl, y_up, c), device(zl, y_dn, c)

    def line(k):
        right = order[k] > zl
        upstream = jnp.where(right, zl > 0, zl < NZ - 1)
        return right, upstream, jnp.where(right, 0, 1)

    def b_rows(y_):
        return pl.ds(pl.multiple_of(y_ * ROWS_B, ROWS_B), ROWS_B)

    def send_line_b(k, cond):
        right, _, side = line(k)
        zd = order[k]
        for step, way in ((1, right), (-1, jnp.logical_not(right))):
            hand(part_b.at[zd], zb_in.at[side, zd], lineb_recv.at[side * NZ + zd], z_dev(step), both(cond, way))

    def send_line_a(k, cond):
        right, _, side = line(k)
        zd = order[k]
        for step, way in ((1, right), (-1, jnp.logical_not(right))):
            hand(part_a.at[zd, y], z_in.at[side, zd], line_recv.at[side * NZ + zd], z_dev(step), both(cond, way))

    def pass_line_b(k):
        _, upstream, side = line(k)
        zd = order[k]
        landed(zb_in.at[side, zd], lineb_recv.at[side * NZ + zd], upstream)

        @pl.when(upstream)
        def _():
            add_to(part_b.at[zd], zb_in.at[side, zd])

        send_line_b(k, upstream)

    def own_line_b():
        for side, there in ((0, zl > 0), (1, zl < NZ - 1)):
            landed(zb_in.at[side, zl], lineb_recv.at[side * NZ + zl], there)

            @pl.when(there)
            def _():
                add_to(part_b.at[zl], zb_in.at[side, zl])

        for dev, way in ((up_dev, even(zl)), (dn_dev, odd(zl))):
            hand(part_b.at[zl, b_rows(y_far)], yb_far_in, farb_recv, dev, way)

    def own_line_a():
        for side, there in ((0, zl > 0), (1, zl < NZ - 1)):
            landed(z_in.at[side, zl], line_recv.at[side * NZ + zl], there)

            @pl.when(there)
            def _():
                weight_grad[0:ROWS_A, :] += z_in[side, zl].astype(f32)

    def ring_b_out():
        landed(yb_far_in, farb_recv)
        add_to(part_b.at[zl, b_rows(jnp.where(even(zl), y_up, y_dn))], yb_far_in)
        hand(part_b.at[zl, b_rows(y_up)], yb_in.at[0], ringb_recv.at[0], up_dev)
        hand(part_b.at[zl, b_rows(y_dn)], yb_in.at[1], ringb_recv.at[1], dn_dev)

    def ring_b_in():
        for side in range(2):
            landed(yb_in.at[side], ringb_recv.at[side])
        weight_grad[ROWS_A:SHARD, :] = (
            part_b[zl, b_rows(y)].astype(f32) + yb_in[0].astype(f32) + yb_in[1].astype(f32)
        )

    def pass_line_a(k):
        _, upstream, side = line(k)
        zd = order[k]
        landed(z_in.at[side, zd], line_recv.at[side * NZ + zd], upstream)

        @pl.when(upstream)
        def _():
            add_to(part_a.at[zd, y], z_in.at[side, zd])

        send_line_a(k, upstream)

    def ring_out(k):
        zd = order[k]
        landed(y_far_in.at[zd], far_recv.at[zd])
        target = jnp.where(even(zd), y_up, y_dn)
        add_to(part_a.at[zd, target], y_far_in.at[zd])
        hand(part_a.at[zd, y_up], y_in.at[zd, 0], ring_recv.at[zd * 2], up_dev)
        hand(part_a.at[zd, y_dn], y_in.at[zd, 1], ring_recv.at[zd * 2 + 1], dn_dev)

    def ring_in(k):
        zd = order[k]
        for side in range(2):
            landed(y_in.at[zd, side], ring_recv.at[zd * 2 + side])
        if k < NZ - 1:
            add_to(part_a.at[zd, y], y_in.at[zd, 0], y_in.at[zd, 1])
            send_line_a(k, jnp.logical_not(line(k)[1]))
        else:
            weight_grad[0:ROWS_A, :] = (
                part_a[zd, y].astype(f32) + y_in[zd, 0].astype(f32) + y_in[zd, 1].astype(f32)
            )

    gain_steps = (
        partner, device(zl, jnp.where(even(y), y + 1, y - 1), c), device(zl, y_far, c),
        device(jnp.where(even(zl), zl + 1, zl - 1), y, c), z_skip,
    )
    gain_buf[0] = jnp.sum(gain_acc[...], axis=0, keepdims=True)

    def gain_copy(k):
        return remote(gain_buf.at[k], gain_buf.at[6 + k], gain_send.at[k], gain_recv.at[k], gain_steps[k])

    def gain_add(k):
        gain_copy(k).wait_recv()
        gain_buf[k + 1] = gain_buf[k] + gain_buf[6 + k]
        if k + 1 < len(gain_steps):
            gain_copy(k + 1).start()

    def produce(k):
        zd = order[k]
        cols = pl.ds(pl.multiple_of(zd * 256, 256), 256)
        total = lax.dot_general(pack[:, cols], dmixed[...], (((0,), (0,)), ((), ())), preferred_element_type=f32).astype(bf16)
        for j in range(NY):
            part_a[zd, j] = total[j * SHARD : j * SHARD + ROWS_A]
            part_b[zd, j * ROWS_B : (j + 1) * ROWS_B] = total[j * SHARD + ROWS_A : (j + 1) * SHARD]
        for dev, way in ((up_dev, even(zd)), (dn_dev, odd(zd))):
            hand(part_a.at[zd, y_far], y_far_in.at[zd], far_recv.at[zd], dev, way)
        if k < NZ - 1:
            send_line_b(k, jnp.logical_not(line(k)[1]))

    produce(0)
    gain_copy(0).start()
    produce(1)
    ring_out(0)
    produce(2)
    pass_line_b(0)
    gain_add(0)
    produce(3)
    ring_out(1)
    pass_line_b(1)
    ring_in(0)
    gain_add(1)
    ring_out(2)
    pass_line_b(2)
    ring_in(1)
    gain_add(2)
    pass_line_a(0)
    own_line_b()
    gain_add(3)
    ring_out(3)
    ring_in(2)
    gain_add(4)
    ring_b_out()
    pass_line_a(1)
    before = len(scatter)
    pass_line_a(2)
    last_hops = len(scatter) - before

    def drain_sums(start, stop):
        for copy, cond in scatter[start:stop]:
            if cond is None:
                copy.wait_send()
            else:
                pl.when(cond)(copy.wait_send)

    ring_in(3)
    ring_b_in()
    lax.fori_loop(0, MICRO, drain_backward, 0)
    pack_copy.wait_send()
    for k in range(len(gain_steps)):
        gain_copy(k).wait_send()
    drain_sums(0, before)
    own_line_a()

    gain_out[...] = gain_buf[5]

    drain_sums(len(scatter) - last_hops, len(scatter))

    @pl.when(s >= OVER)
    def _():
        lax.fori_loop(0, MICRO, drain_forward, 0)


def hand_over(*refs):
    n = len(refs) // 2
    copies = []
    for src, dst in zip(refs[:n], refs[n : 2 * n]):
        rows = src.shape[0]
        pieces = 8 if rows * src.shape[1] >= 2**17 else 1
        for k in range(pieces):
            part = pl.ds(k * (rows // pieces), rows // pieces)
            copies.append(pltpu.make_async_copy(src.at[part], dst.at[part], refs[-1].at[len(copies)]))
    for copy in copies:
        copy.start()
    for copy in copies:
        copy.wait()


def body(first_input, upstream, history, example_ids, norm_gain, weight):
    vmem = pl.BlockSpec(memory_space=pltpu.VMEM)
    anywhere = pl.BlockSpec(memory_space=pl.ANY)
    smem = pl.BlockSpec(memory_space=pltpu.SMEM)
    dma = pltpu.SemaphoreType.DMA
    out, scales, weight_grad, gain_grad = pl.pallas_call(
        relay_kernel,
        out_shape=(
            jax.ShapeDtypeStruct((TOK, D), bf16),
            jax.ShapeDtypeStruct((D // BLOCK, TOK), bf16),
            jax.ShapeDtypeStruct((SHARD, D), f32),
            jax.ShapeDtypeStruct((1, D), f32),
        ),
        in_specs=[anywhere, anywhere, anywhere, smem, vmem, anywhere],
        out_specs=(vmem,) * 4,
        scratch_shapes=[
            pltpu.VMEM((NZ, NY, 2, SHARD, D), bf16),
            pltpu.VMEM((D, D), bf16),
            pltpu.VMEM((4, SEQ, D), bf16),
            pltpu.VMEM((TOK, D), bf16),
            pltpu.VMEM((TOK, D), bf16),
            pltpu.VMEM((TOK, D), bf16),
            pltpu.VMEM((TOK, D), bf16),
            pltpu.VMEM((TOK, HALF), bf16),
            pltpu.VMEM((TOK, HALF), bf16),
            pltpu.VMEM((TOK, D), f32),
            pltpu.VMEM((TOK, D), bf16),
            pltpu.VMEM((TOK, BLOCK), f32),
            pltpu.VMEM((WIDE, D), f32),
            pltpu.VMEM((TOK, BLOCK), f32),
            pltpu.VMEM((8, D), f32),
            pltpu.VMEM((11, 1, D), f32),
            pltpu.VMEM((2 * TOK, HALF), bf16),
            pltpu.VMEM((TOK, HALF), bf16),
            pltpu.VMEM((2 * TOK, D), bf16),
            pltpu.VMEM((NZ, NY, ROWS_A, D), bf16),
            pltpu.VMEM((NZ, NY * ROWS_B, D), bf16),
            pltpu.VMEM((NZ, ROWS_A, D), bf16),
            pltpu.VMEM((NZ, 2, ROWS_A, D), bf16),
            pltpu.VMEM((2, NZ, ROWS_A, D), bf16),
            pltpu.VMEM((2, NZ, NY * ROWS_B, D), bf16),
            pltpu.VMEM((ROWS_B, D), bf16),
            pltpu.VMEM((2, ROWS_B, D), bf16),
            dma((4,)),
            dma((MICRO,)), dma((MICRO,)), dma((MICRO,)), dma((MICRO,)),
            dma((MICRO,)), dma((MICRO,)), dma((MICRO,)), dma((MICRO,)),
            dma((NZ,)), dma((NZ * NY,)), dma((NY,)), dma((NZ * NY,)), dma(()), dma((136,)),
            dma((2,)), dma((MICRO,)), dma((MICRO,)), dma((5,)), dma((5,)),
            dma((96,)), dma((NZ,)), dma((NZ * 2,)), dma((2 * NZ,)), dma((2 * NZ,)), dma(()), dma((2,)),
        ],
        compiler_params=pltpu.CompilerParams(
            collective_id=0, has_side_effects=True, vmem_limit_bytes=56 * 2**20
        ),
    )(first_input, upstream, history, example_ids, norm_gain, weight)
    results = (out, scales, weight_grad, gain_grad)
    out, scales, weight_grad, gain_grad = pl.pallas_call(
        hand_over,
        out_shape=tuple(jax.ShapeDtypeStruct(r.shape, r.dtype) for r in results),
        in_specs=[vmem] * 4,
        out_specs=(anywhere,) * 4,
        scratch_shapes=[dma((18,))],
    )(*results)
    return (out[None], scales.T[None], weight_grad[None], gain_grad)


def solution(mesh):
    return jax.shard_map(
        body,
        mesh=mesh,
        in_specs=(
            P("dp", None),
            P("dp", None),
            P("section", None, "dp", None, None),
            P("dp", None),
            P("section", None),
            P("section", "dp", None),
        ),
        out_specs=(
            P("section", "dp", None),
            P("section", "dp", None),
            P("section", "dp", None),
            P("section", None),
        ),
        check_vma=False,
    )
```
